32 devices in a mesh: band: 4 (over z), trial: 8 (over y, x, core).
Axes of the slice: x: 2, y: 2, z: 4, core: 2. Of those that a mesh axis runs over, the one named last changes fastest.
Arguments:
- intensity: bfloat16 [2, 16384, 2048], P(None, 'band', 'trial'), may hold values from -6 to 6
- fine_delay: int32 [32, 32, 512], P('band'), may hold values from 0 to 31
- span_start: int32 [8, 32], replicated, may hold values from 0 to 28
- sub_rel: int32 [512, 32], P('trial'), may hold values from 0 to 3
- offset: int32 [512, 32], P('trial'), may hold values from 0 to 1024
- widths: int32 [4], replicated, may hold values from 1 to 64
Outputs:
- series: bfloat16 [2, 512, 2048], P(None, ('trial', 'band'))
- peaks: float32 [2, 512, 4], P(None, ('trial', 'band'))
The draws below stay inside these ranges and needn't reach their ends.
All inputs are finite; a program needn't handle non-finite values.
Results may differ from the reference program's by a relative error of at most 0.014.
Values may be sent and summed in bfloat16 or wider, within the bound.
No kernel may reach another device: no remote copies, remote signals or barrier semaphores. Data moves between devices by JAX's collectives and lax.ppermute only.
A program may use at most 64 MiB of HBM per device.

```python
import math
import jax
import jax.numpy as jnp
from jax import lax

BEAMS = 2
CH = 16384
SUBS = 32
CSUB = 512
Q = 32
QSPAN = 4
MAXD1 = 32
TIME = 2048
MAXD2 = 1024
TRIAL_DEV = 64
TRIALS = 512
NW = 4
MAXW = 64
N_TRIAL = 8


def plant(values, own_key, smallest, largest):
    spot = [jax.random.randint(jax.random.fold_in(own_key, axis), (), 0, length) for axis, length in enumerate(values.shape)]
    widest = values.shape.index(max(values.shape))
    beside = spot[:widest] + [(spot[widest] + 1) % values.shape[widest]] + spot[widest + 1:]
    return values.at[tuple(spot)].set(smallest).at[tuple(beside)].set(largest)


def shard_levels(key, dims, cuts, smallest, top_value):
    factor_of = 1.0
    for axis_at, blocks in cuts:
        steps = jax.random.uniform(jax.random.fold_in(jax.random.fold_in(key, 6), axis_at), (blocks,), jnp.float32, smallest / len(cuts), top_value / len(cuts))
        factor_of = factor_of * jnp.repeat(jnp.exp(steps), dims[axis_at] // blocks).reshape((-1,) + (1,) * (len(dims) - 1 - axis_at))
    return factor_of


def gaussian(rng, dims, deviation, reach, pieces=(), kind=jnp.bfloat16):
    drawn = jax.random.normal(rng, dims, jnp.float32) * deviation
    if len(pieces) > 0:
        drawn = shard_levels(rng, dims, pieces, -0.22, 0.18) * drawn
    return jnp.clip(drawn, min=-reach, max=reach).astype(kind)


def setup_inputs(seed: int = 0) -> dict:
    key_of = jax.random.split(jax.random.key(seed), 7)
    intensity = gaussian(key_of[0], (BEAMS, CH, TIME), 1.0, 6.0, ((1, 4), (2, 8)))
    fine_delay = plant(jax.random.randint(key_of[1], (SUBS, Q, CSUB), 0, MAXD1), jax.random.fold_in(key_of[1], 1), 0, MAXD1 - 1).astype(jnp.int32)
    span_start = plant(jax.random.randint(key_of[2], (N_TRIAL, SUBS), 0, Q - QSPAN + 1), jax.random.fold_in(key_of[2], 1), 0, Q - QSPAN).astype(jnp.int32)
    sub_rel = plant(jax.random.randint(key_of[3], (TRIALS, SUBS), 0, QSPAN), jax.random.fold_in(key_of[3], 1), 0, QSPAN - 1).astype(jnp.int32)
    offset = plant(jax.random.randint(key_of[4], (TRIALS, SUBS), 0, MAXD2 + 1), jax.random.fold_in(key_of[4], 1), 0, MAXD2).astype(jnp.int32)
    widths = plant(jax.random.randint(key_of[5], (NW,), 1, MAXW + 1), jax.random.fold_in(key_of[5], 1), 1, MAXW).astype(jnp.int32)
    return {"intensity": intensity, "fine_delay": fine_delay, "span_start": span_start, "sub_rel": sub_rel, "offset": offset, "widths": widths}


def boxcar_peaks(series, widths):
    values = series.astype(jnp.float32)
    length = values.shape[2]
    running = jnp.cumsum(values, axis=2)
    start_zero = jnp.zeros(values.shape[:2] + (1,), jnp.float32)
    tail_sums = jnp.broadcast_to(running[:, :, -1:], values.shape[:2] + (MAXW,))
    prefix_sums = jnp.concatenate([start_zero, running, tail_sums], axis=2)
    peak_list = []
    for width_slot in range(widths.shape[0]):
        width_now = widths[width_slot]
        upper_sums = lax.dynamic_slice_in_dim(prefix_sums, width_now, length, 2)
        boxcar_sums = (upper_sums - prefix_sums[:, :, :length]) / jnp.sqrt(width_now.astype(jnp.float32))
        peak_list.append(lax.optimization_barrier(jnp.max(boxcar_sums, axis=2)))
    return jnp.stack(peak_list, axis=2)

def reference(intensity, fine_delay, span_start, sub_rel, offset, widths):
    blocks = intensity.reshape(BEAMS, SUBS, CSUB, TIME).transpose(1, 0, 2, 3)

    def sub_band(operands):
        block_data, delays = operands
        extended = jnp.pad(block_data.astype(jnp.float32), ((0, 0), (0, 0), (0, MAXD1)))
        summed_band = jnp.zeros((BEAMS, Q, TIME), jnp.float32)
        for delay_step in range(MAXD1):
            selector = (delays == delay_step).astype(jnp.float32)
            summed_band = summed_band + jnp.einsum('qc,bct->bqt', selector, extended[:, :, delay_step:delay_step + TIME], precision=lax.Precision.HIGHEST)
        return summed_band.astype(jnp.bfloat16)
    partial_rows = lax.map(sub_band, (blocks, fine_delay))
    padded = jnp.pad(partial_rows, ((0, 0), (0, 0), (0, 0), (0, MAXD2)))
    trial_range = jnp.arange(TRIALS, dtype=jnp.int32) // TRIAL_DEV
    sub_trial = (span_start[trial_range] + sub_rel).astype(jnp.int32)
    band_index = jnp.arange(SUBS, dtype=jnp.int32)

    def select(band_id, row_start, time_shift):
        zero_index = jnp.zeros((), jnp.int32)
        picked = lax.dynamic_slice(padded, (band_id, zero_index, row_start, time_shift), (1, BEAMS, 1, TIME))
        return picked[0, :, 0].astype(jnp.float32)

    def one_trial(rows_one, shifts_one):
        return lax.optimization_barrier(jnp.sum(jax.vmap(select)(band_index, rows_one, shifts_one), axis=0))
    groups = TRIALS // 8

    def trial_group(operands):
        return jax.vmap(one_trial)(operands[0], operands[1])
    summed = lax.map(trial_group, (sub_trial.reshape(groups, 8, SUBS), offset.reshape(groups, 8, SUBS)))
    summed = summed.reshape(TRIALS, BEAMS, TIME).transpose(1, 0, 2)
    series = (summed / math.sqrt(CH)).astype(jnp.bfloat16)
    return (series, boxcar_peaks(series, widths))
```

```python
import functools
import math

import jax
import jax.numpy as jnp
from jax import lax
from jax.experimental import pallas as pl
from jax.experimental.pallas import tpu as pltpu
from jax.sharding import PartitionSpec as P

QSPAN = 4
MAXD1 = 32
LANES = 128


def round_up(number, step):
    return (number + step - 1) // step * step


def fine_kernel(subs, trials_axis, rows, span_ref, x_ref, delay_ref, out_ref, lagged_ref, part_ref, send_ref):
    sub = pl.program_id(0)
    beams, width, block_len = x_ref.shape
    q_count = delay_ref.shape[1]
    halves = block_len // LANES
    lane = lax.broadcasted_iota(jnp.int32, (8, LANES), 1)
    delays = delay_ref[0]
    selector = jnp.concatenate(
        [(delays == lag).astype(jnp.bfloat16) for lag in range(MAXD1)], axis=0
    )
    for beam in range(beams):
        lagged_ref[...] = jnp.dot(selector, x_ref[beam], preferred_element_type=jnp.float32)
        for group in range(q_count // 8):
            sums = [jnp.zeros((8, LANES), jnp.float32) for _ in range(halves + 1)]
            for lag in range(MAXD1):
                base = lag * q_count + group * 8
                for half in range(halves):
                    piece = lagged_ref[base : base + 8, half * LANES : (half + 1) * LANES]
                    if lag == 0:
                        sums[half + 1] = sums[half + 1] + piece
                        continue
                    moved = pltpu.roll(piece, LANES - lag, 1)
                    stays = lane < LANES - lag
                    sums[half + 1] = sums[half + 1] + jnp.where(stays, moved, 0.0)
                    sums[half] = sums[half] + jnp.where(stays, 0.0, moved)
            before = sums[0]
            before = before + pltpu.roll(before, 32, 1)
            sums[0] = before + pltpu.roll(before, 64, 1)
            for piece in range(halves + 1):
                part_ref[beam, piece, group * 8 : group * 8 + 8, :] = sums[piece]
    own = lax.axis_index("band") * subs + sub
    row_id = lax.broadcasted_iota(jnp.int32, (QSPAN, LANES), 0)
    lane_part = lax.broadcasted_iota(jnp.int32, (QSPAN, LANES), 1) // MAXD1
    main = subs * beams * halves * QSPAN
    for target in range(trials_axis):
        start = span_ref[target, own]
        for beam in range(beams):
            for half in range(halves):
                place = (sub * beams + beam) * halves * QSPAN + half * QSPAN
                send_ref[pl.ds(target * rows + place, QSPAN), :] = part_ref[
                    beam, half + 1, pl.ds(start, QSPAN), :
                ]
            tails = part_ref[beam, 0, pl.ds(start, QSPAN), :]
            tails = jnp.sum(jnp.where(row_id == lane_part, tails, 0.0), axis=0, keepdims=True)
            send_ref[pl.ds(target * rows + main + sub * beams + beam, 1), :] = tails

    @pl.when(sub == subs - 1)
    def _():
        for target in range(trials_axis):
            out_ref[target] = send_ref[target * rows : (target + 1) * rows].astype(jnp.bfloat16)


def trial_kernel(subs, beams, bands, rel_ref, offset_ref, recv_ref, out_ref, flat_ref, wide_ref, sums_ref):
    sources, rows, _ = recv_ref.shape
    trials = rel_ref.shape[0]
    halves = 2
    blocks = sources * halves
    stride = wide_ref.shape[1]
    main = subs * beams * halves * QSPAN
    lane = lax.broadcasted_iota(jnp.int32, (8, LANES), 1)
    for source in range(sources):
        flat_ref[source * rows : (source + 1) * rows] = recv_ref[source].astype(jnp.float32)
    flat_ref[sources * rows :] = jnp.zeros((rows, LANES), jnp.float32)
    lane_all = lax.broadcasted_iota(jnp.int32, (sources, LANES), 1)
    for sub in range(subs):
        for beam in range(beams):
            pair = sub * beams + beam
            tails = flat_ref[pl.ds(rows + main + pair, sources, stride=rows), :]
            for span in range(QSPAN):
                row = pair * QSPAN + span
                wide_ref[row, blocks:, :] = jnp.zeros((stride - blocks, LANES), jnp.float32)
                for half in range(halves):
                    piece = flat_ref[
                        pl.ds(pair * halves * QSPAN + half * QSPAN + span, sources, stride=rows), :
                    ]
                    if half == halves - 1:
                        turn = (LANES - MAXD1 - span * MAXD1) % LANES
                        moved = pltpu.roll(tails, turn, 1) if turn else tails
                        piece = piece + jnp.where(lane_all >= LANES - MAXD1, moved, 0.0)
                    wide_ref[row, pl.ds(half, sources, stride=halves), :] = piece
    first = lax.axis_index("band") * subs
    per_band = trials // bands
    step_rows = beams * per_band

    def one_trial(trial, carry):
        sums = [[jnp.zeros((8, LANES), jnp.float32) for _ in range(blocks // 8)] for _ in range(beams)]
        for sub in range(subs):
            span = rel_ref[trial, first + sub]
            shift = offset_ref[trial, first + sub]
            coarse = shift // LANES
            fine = shift - coarse * LANES
            keep = lane >= fine
            turn = (LANES - fine) % LANES
            for beam in range(beams):
                row = (sub * beams + beam) * QSPAN + span
                for part in range(blocks // 8):
                    near = wide_ref[row, pl.ds(coarse + part * 8, 8), :]
                    far = wide_ref[row, pl.ds(coarse + part * 8 + 1, 8), :]
                    moved = pltpu.roll(jnp.where(keep, near, far), turn, 1)
                    sums[beam][part] = sums[beam][part] + moved
        band = trial // per_band
        inside = trial - band * per_band
        for beam in range(beams):
            for part in range(blocks // 8):
                start = (band * blocks + part * 8) * step_rows + beam * per_band + inside
                sums_ref[pl.ds(start, 8, stride=step_rows), :] = sums[beam][part]
        return carry

    lax.fori_loop(0, trials, one_trial, 0)
    out_ref[...] = sums_ref[...].astype(jnp.bfloat16)


def peak_kernel(beams, scale, width_ref, x_ref, series_ref, peak_ref):
    blocks, rows, _ = x_ref.shape
    per_beam = rows // beams
    series = [(x_ref[block].astype(jnp.float32) / scale).astype(jnp.bfloat16) for block in range(blocks)]
    for block in range(blocks):
        for beam in range(beams):
            series_ref[beam, :, block * LANES : (block + 1) * LANES] = (
                series[block].astype(jnp.float32)[beam * per_beam : (beam + 1) * per_beam].astype(jnp.bfloat16)
            )
    following = series[1:] + [jnp.zeros_like(series[0])]
    left = jnp.concatenate(
        [jnp.concatenate([here, after], axis=1) for here, after in zip(series, following)], axis=0
    )
    source = lax.broadcasted_iota(jnp.int32, (2 * LANES, LANES), 0)
    place = lax.broadcasted_iota(jnp.int32, (2 * LANES, LANES), 1)
    slot_id = lax.broadcasted_iota(jnp.int32, (rows, peak_ref.shape[2]), 1)
    peaks = jnp.zeros((rows, peak_ref.shape[2]), jnp.float32)
    for slot in range(peak_ref.shape[2]):
        width = width_ref[slot]
        window = ((source >= place) & (source < place + width)).astype(jnp.bfloat16)
        totals = jnp.dot(left, window, preferred_element_type=jnp.float32)
        best = totals[:rows]
        for block in range(1, blocks):
            best = jnp.maximum(best, totals[block * rows : (block + 1) * rows])
        best = jnp.max(best, axis=1, keepdims=True)
        root = jnp.sqrt(jnp.full((rows, 1), width, jnp.int32).astype(jnp.float32))
        peaks = jnp.where(slot_id == slot, best / root, peaks)
    for beam in range(beams):
        peak_ref[beam] = peaks[beam * per_beam : (beam + 1) * per_beam]


def local(intensity, fine_delay, span_start, sub_rel, offset, widths):
    beams, channels, block_len = intensity.shape
    subs, q_count, width = fine_delay.shape
    sources = lax.axis_size("trial")
    bands = lax.axis_size("band")
    trials = sub_rel.shape[0]
    halves = block_len // LANES
    blocks = sources * halves
    length = sources * block_len
    main = subs * beams * halves * QSPAN
    rows = round_up(main + subs * beams, 16)
    send = pl.pallas_call(
        functools.partial(fine_kernel, subs, sources, rows),
        grid_spec=pltpu.PrefetchScalarGridSpec(
            num_scalar_prefetch=1,
            grid=(subs,),
            in_specs=[
                pl.BlockSpec((beams, width, block_len), lambda sub, span: (0, sub, 0)),
                pl.BlockSpec((1, q_count, width), lambda sub, span: (sub, 0, 0)),
            ],
            out_specs=pl.BlockSpec((sources, rows, LANES), lambda sub, span: (0, 0, 0)),
            scratch_shapes=[
                pltpu.VMEM((MAXD1 * q_count, block_len), jnp.float32),
                pltpu.VMEM((beams, halves + 1, q_count, LANES), jnp.float32),
                pltpu.VMEM((sources * rows, LANES), jnp.float32),
            ],
        ),
        out_shape=jax.ShapeDtypeStruct((sources, rows, LANES), jnp.bfloat16),
        compiler_params=pltpu.CompilerParams(vmem_limit_bytes=48 << 20),
        name="fine_delays",
    )(span_start, intensity, fine_delay)
    received = lax.all_to_all(send, "trial", split_axis=0, concat_axis=0, tiled=True)
    stride = round_up(blocks + length // 2 // LANES + 1, 8)
    per_band = trials // bands
    sums = pl.pallas_call(
        functools.partial(trial_kernel, subs, beams, bands),
        in_specs=[
            pl.BlockSpec(memory_space=pltpu.SMEM),
            pl.BlockSpec(memory_space=pltpu.SMEM),
            pl.BlockSpec(memory_space=pltpu.VMEM),
        ],
        out_specs=pl.BlockSpec(memory_space=pltpu.VMEM),
        scratch_shapes=[
            pltpu.VMEM(((sources + 1) * rows, LANES), jnp.float32),
            pltpu.VMEM((subs * beams * QSPAN, stride, LANES), jnp.float32),
            pltpu.VMEM((blocks * beams * trials, LANES), jnp.float32),
        ],
        out_shape=jax.ShapeDtypeStruct((blocks * beams * trials, LANES), jnp.bfloat16),
        compiler_params=pltpu.CompilerParams(vmem_limit_bytes=48 << 20),
        name="trial_sums",
    )(sub_rel, offset, received)
    summed = lax.psum_scatter(sums, "band", scatter_dimension=0, tiled=True)
    summed = summed.reshape(blocks, beams * per_band, LANES)
    return pl.pallas_call(
        functools.partial(peak_kernel, beams, math.sqrt(channels * bands)),
        in_specs=[
            pl.BlockSpec(memory_space=pltpu.SMEM),
            pl.BlockSpec(memory_space=pltpu.VMEM),
        ],
        out_specs=[pl.BlockSpec(memory_space=pltpu.VMEM)] * 2,
        out_shape=[
            jax.ShapeDtypeStruct((beams, per_band, length), jnp.bfloat16),
            jax.ShapeDtypeStruct((beams, per_band, widths.shape[0]), jnp.float32),
        ],
        compiler_params=pltpu.CompilerParams(vmem_limit_bytes=48 << 20),
        name="boxcar_peaks",
    )(widths, summed)


def solution(mesh):
    return jax.shard_map(
        lambda *arrays: tuple(local(*arrays)),
        mesh=mesh,
        in_specs=(
            P(None, "band", "trial"),
            P("band", None, None),
            P(),
            P("trial", None),
            P("trial", None),
            P(),
        ),
        out_specs=(P(None, ("trial", "band"), None), P(None, ("trial", "band"), None)),
        check_vma=False,
    )
```

```python
import functools
import math

import jax
import jax.numpy as jnp
from jax import lax
from jax.experimental import pallas as pl
from jax.experimental.pallas import tpu as pltpu
from jax.sharding import PartitionSpec as P

QSPAN = 4
MAXD1 = 32
LANES = 128


def round_up(number, step):
    return (number + step - 1) // step * step


def fine_kernel(subs, trials_axis, rows, span_ref, x_ref, delay_ref, out_ref, lagged_ref, part_ref, send_ref):
    sub = pl.program_id(0)
    beams, width, block_len = x_ref.shape
    q_count = delay_ref.shape[1]
    halves = block_len // LANES
    lane = lax.broadcasted_iota(jnp.int32, (8, LANES), 1)
    delays = delay_ref[0]
    selector = jnp.concatenate(
        [(delays == lag).astype(jnp.bfloat16) for lag in range(MAXD1)], axis=0
    )
    for beam in range(beams):
        lagged_ref[...] = jnp.dot(selector, x_ref[beam], preferred_element_type=jnp.float32)
        for group in range(q_count // 8):
            sums = [jnp.zeros((8, LANES), jnp.float32) for _ in range(halves + 1)]
            for lag in range(MAXD1):
                base = lag * q_count + group * 8
                for half in range(halves):
                    piece = lagged_ref[base : base + 8, half * LANES : (half + 1) * LANES]
                    if lag == 0:
                        sums[half + 1] = sums[half + 1] + piece
                        continue
                    moved = pltpu.roll(piece, LANES - lag, 1)
                    stays = lane < LANES - lag
                    sums[half + 1] = sums[half + 1] + jnp.where(stays, moved, 0.0)
                    sums[half] = sums[half] + jnp.where(stays, 0.0, moved)
            before = sums[0]
            before = before + pltpu.roll(before, 32, 1)
            sums[0] = before + pltpu.roll(before, 64, 1)
            for piece in range(halves + 1):
                part_ref[beam, piece, group * 8 : group * 8 + 8, :] = sums[piece]
    own = lax.axis_index("band") * subs + sub
    row_id = lax.broadcasted_iota(jnp.int32, (QSPAN, LANES), 0)
    lane_part = lax.broadcasted_iota(jnp.int32, (QSPAN, LANES), 1) // MAXD1
    main = subs * beams * halves * QSPAN
    for target in range(trials_axis):
        start = span_ref[target, own]
        for beam in range(beams):
            for half in range(halves):
                place = (sub * beams + beam) * halves * QSPAN + half * QSPAN
                send_ref[pl.ds(target * rows + place, QSPAN), :] = part_ref[
                    beam, half + 1, pl.ds(start, QSPAN), :
                ]
            tails = part_ref[beam, 0, pl.ds(start, QSPAN), :]
            tails = jnp.sum(jnp.where(row_id == lane_part, tails, 0.0), axis=0, keepdims=True)
            send_ref[pl.ds(target * rows + main + sub * beams + beam, 1), :] = tails

    @pl.when(sub == subs - 1)
    def _():
        for target in range(trials_axis):
            out_ref[target] = send_ref[target * rows : (target + 1) * rows].astype(jnp.bfloat16)


def spread(subs, beams, recv_ref, wide_ref, flat_ref):
    sources, rows, _ = recv_ref.shape
    halves = 2
    blocks = sources * halves
    main = subs * beams * halves * QSPAN
    for source in range(sources):
        flat_ref[source * rows : (source + 1) * rows] = recv_ref[source].astype(jnp.float32)
    flat_ref[sources * rows :] = jnp.zeros((rows, LANES), jnp.float32)
    lane = lax.broadcasted_iota(jnp.int32, (sources, LANES), 1)
    for pair in range(subs * beams):
        tails = flat_ref[pl.ds(rows + main + pair, sources, stride=rows), :]
        for span in range(QSPAN):
            row = pair * QSPAN + span
            wide_ref[row, blocks:, :] = jnp.zeros((wide_ref.shape[1] - blocks, LANES), jnp.float32)
            for half in range(halves):
                place = pair * halves * QSPAN + half * QSPAN + span
                piece = flat_ref[pl.ds(place, sources, stride=rows), :]
                if half == halves - 1:
                    turn = (LANES - MAXD1 - span * MAXD1) % LANES
                    moved = pltpu.roll(tails, turn, 1) if turn else tails
                    piece = piece + jnp.where(lane >= LANES - MAXD1, moved, 0.0)
                wide_ref[row, pl.ds(half, sources, stride=halves), :] = piece


def add_trials(subs, beams, first, count, place_ref, wide_ref, sums_ref):
    blocks = sums_ref.shape[0] // (beams * count)
    lane = lax.broadcasted_iota(jnp.int32, (8, LANES), 1)

    def one_trial(inside, carry):
        sums = [[None] * (blocks // 8) for _ in range(beams)]
        for sub in range(subs):
            place = place_ref[sub, first + inside]
            row = place >> 20
            coarse = (place >> 7) & 0x1FFF
            fine = place & (LANES - 1)
            keep = lane >= fine
            turn = (LANES - fine) & (LANES - 1)
            for beam in range(beams):
                for part in range(blocks // 8):
                    at = coarse + part * 8
                    near = wide_ref[row + beam * QSPAN, pl.ds(at, 8), :]
                    far = wide_ref[row + beam * QSPAN, pl.ds(at + 1, 8), :]
                    moved = pltpu.roll(jnp.where(keep, near, far), turn, 1)
                    held = sums[beam][part]
                    sums[beam][part] = moved if held is None else held + moved
        for beam in range(beams):
            for part in range(blocks // 8):
                start = part * 8 * beams * count + beam * count + inside
                sums_ref[pl.ds(start, 8, stride=beams * count), :] = sums[beam][part]
        return carry

    lax.fori_loop(0, count, one_trial, 0, unroll=2)


def partner(place, step, peers):
    return place ^ step if peers & (peers - 1) == 0 else (place + step) % peers


def first_kernel(subs, beams, bands, step, count, place_ref, recv_ref, wide_ref, out_ref, flat_ref, sums_ref):
    spread(subs, beams, recv_ref, wide_ref, flat_ref)
    band = partner(lax.axis_index("band"), step, bands)
    add_trials(subs, beams, band * count, count, place_ref, wide_ref, sums_ref)
    out_ref[...] = sums_ref[...].reshape(out_ref.shape).astype(out_ref.dtype)


def next_kernel(subs, beams, bands, step, count, place_ref, wide_ref, out_ref, sums_ref):
    band = partner(lax.axis_index("band"), step, bands)
    add_trials(subs, beams, band * count, count, place_ref, wide_ref, sums_ref)
    out_ref[...] = sums_ref[...].reshape(out_ref.shape).astype(out_ref.dtype)


def peak_kernel(beams, scale, width_ref, *refs):
    x_refs, (series_ref, peak_ref) = refs[:-2], refs[-2:]
    blocks, rows, _ = x_refs[0].shape
    per_beam = rows // beams
    series = []
    for block in range(blocks):
        total = x_refs[0][block].astype(jnp.float32)
        for x_ref in x_refs[1:]:
            total = total + x_ref[block].astype(jnp.float32)
        series.append((total / scale).astype(jnp.bfloat16))
    for block in range(blocks):
        for beam in range(beams):
            series_ref[beam, :, block * LANES : (block + 1) * LANES] = (
                series[block].astype(jnp.float32)[beam * per_beam : (beam + 1) * per_beam].astype(jnp.bfloat16)
            )
    following = series[1:] + [jnp.zeros_like(series[0])]
    left = jnp.concatenate(
        [jnp.concatenate([here, after], axis=1) for here, after in zip(series, following)], axis=0
    )
    source = lax.broadcasted_iota(jnp.int32, (2 * LANES, LANES), 0)
    place = lax.broadcasted_iota(jnp.int32, (2 * LANES, LANES), 1)
    slot_id = lax.broadcasted_iota(jnp.int32, (rows, peak_ref.shape[2]), 1)
    peaks = jnp.zeros((rows, peak_ref.shape[2]), jnp.float32)
    for slot in range(peak_ref.shape[2]):
        width = width_ref[slot]
        window = ((source >= place) & (source < place + width)).astype(jnp.bfloat16)
        totals = jnp.dot(left, window, preferred_element_type=jnp.float32)
        best = totals[:rows]
        for block in range(1, blocks):
            best = jnp.maximum(best, totals[block * rows : (block + 1) * rows])
        best = jnp.max(best, axis=1, keepdims=True)
        root = jnp.sqrt(jnp.full((rows, 1), width, jnp.int32).astype(jnp.float32))
        peaks = jnp.where(slot_id == slot, best / root, peaks)
    for beam in range(beams):
        peak_ref[beam] = peaks[beam * per_beam : (beam + 1) * per_beam]


def local(intensity, fine_delay, span_start, sub_rel, offset, widths):
    beams, channels, block_len = intensity.shape
    subs, q_count, width = fine_delay.shape
    sources = lax.axis_size("trial")
    bands = lax.axis_size("band")
    trials = sub_rel.shape[0]
    halves = block_len // LANES
    blocks = sources * halves
    length = sources * block_len
    main = subs * beams * halves * QSPAN
    rows = round_up(main + subs * beams, 16)
    send = pl.pallas_call(
        functools.partial(fine_kernel, subs, sources, rows),
        grid_spec=pltpu.PrefetchScalarGridSpec(
            num_scalar_prefetch=1,
            grid=(subs,),
            in_specs=[
                pl.BlockSpec((beams, width, block_len), lambda sub, span: (0, sub, 0)),
                pl.BlockSpec((1, q_count, width), lambda sub, span: (sub, 0, 0)),
            ],
            out_specs=pl.BlockSpec((sources, rows, LANES), lambda sub, span: (0, 0, 0)),
            scratch_shapes=[
                pltpu.VMEM((MAXD1 * q_count, block_len), jnp.float32),
                pltpu.VMEM((beams, halves + 1, q_count, LANES), jnp.float32),
                pltpu.VMEM((sources * rows, LANES), jnp.float32),
            ],
        ),
        out_shape=jax.ShapeDtypeStruct((sources, rows, LANES), jnp.bfloat16),
        name="fine_delays",
    )(span_start, intensity, fine_delay)
    own = lax.axis_index("band") * subs
    own_rel = lax.dynamic_slice_in_dim(sub_rel.T, own, subs, 0)
    own_shift = lax.dynamic_slice_in_dim(offset.T, own, subs, 0)
    pair = jnp.arange(subs, dtype=jnp.int32)[:, None] * beams
    places = ((pair * QSPAN + own_rel) << 20) + own_shift
    received = lax.all_to_all(send, "trial", split_axis=0, concat_axis=0, tiled=True)
    stride = round_up(blocks + length // 2 // LANES + 1, 8)
    count = trials // bands
    in_smem = pl.BlockSpec(memory_space=pltpu.SMEM)
    in_vmem = pl.BlockSpec(memory_space=pltpu.VMEM)
    wide_shape = (subs * beams * QSPAN, stride, LANES)
    chunk_shape = (blocks, beams * count, LANES)
    sums_scratch = pltpu.VMEM((blocks * beams * count, LANES), jnp.float32)
    steps = list(range(bands - 1, 0, -1))
    wide = None
    arrived = []
    for step in steps + [0]:
        chunk = jax.ShapeDtypeStruct(chunk_shape, jnp.bfloat16 if step else jnp.float32)
        if wide is None:
            wide, sums = pl.pallas_call(
                functools.partial(first_kernel, subs, beams, bands, step, count),
                in_specs=[in_smem, in_vmem],
                out_specs=[in_vmem, in_vmem],
                scratch_shapes=[pltpu.VMEM(((sources + 1) * rows, LANES), jnp.float32), sums_scratch],
                out_shape=[jax.ShapeDtypeStruct(wide_shape, jnp.float32), chunk],
                name="spread_and_add",
            )(places, received)
        else:
            sums = pl.pallas_call(
                functools.partial(next_kernel, subs, beams, bands, step, count),
                in_specs=[in_smem, in_vmem],
                out_specs=in_vmem,
                scratch_shapes=[sums_scratch],
                out_shape=chunk,
                name="add_trials",
            )(places, wide)
        if step:
            pairs = [(place, partner(place, step, bands)) for place in range(bands)]
            sums = lax.ppermute(sums, "band", pairs)
        arrived.append(sums)
    return pl.pallas_call(
        functools.partial(peak_kernel, beams, math.sqrt(channels * bands)),
        in_specs=[in_smem] + [in_vmem] * bands,
        out_specs=[in_vmem] * 2,
        out_shape=[
            jax.ShapeDtypeStruct((beams, count, length), jnp.bfloat16),
            jax.ShapeDtypeStruct((beams, count, widths.shape[0]), jnp.float32),
        ],
        name="boxcar_peaks",
    )(widths, *arrived[::-1])


def solution(mesh):
    return jax.shard_map(
        lambda *arrays: tuple(local(*arrays)),
        mesh=mesh,
        in_specs=(
            P(None, "band", "trial"),
            P("band", None, None),
            P(),
            P("trial", None),
            P("trial", None),
            P(),
        ),
        out_specs=(P(None, ("trial", "band"), None), P(None, ("trial", "band"), None)),
        check_vma=False,
    )
```

```python
import functools
import math

import jax
import jax.numpy as jnp
from jax import lax
from jax.experimental import pallas as pl
from jax.experimental.pallas import tpu as pltpu
from jax.sharding import PartitionSpec as P

QSPAN = 4
MAXD1 = 32
LANES = 128


def round_up(number, step):
    return (number + step - 1) // step * step


def fine_kernel(trial_ranges, span_ref, x_hbm, delay_ref, out_ref, x_ref, lagged_ref, joined_ref, tail_ref, sems):
    subs, beams, width, block_len = x_ref.shape
    q_count = delay_ref.shape[1]
    packed = LANES // q_count
    tiles = MAXD1 // packed
    halves = block_len // LANES
    reach = MAXD1 + block_len
    unit = trial_ranges * QSPAN * packed
    per_range = QSPAN * packed
    copies = [
        pltpu.make_async_copy(x_hbm.at[:, pl.ds(sub * width, width), :], x_ref.at[sub], sems.at[sub])
        for sub in range(subs)
    ]
    for copy in copies:
        copy.start()
    for beam in range(beams):
        lagged_ref[beam, :MAXD1, :] = jnp.zeros((MAXD1, MAXD1 * q_count), jnp.float32)
        lagged_ref[beam, reach:, :] = jnp.zeros((MAXD1, MAXD1 * q_count), jnp.float32)
    joined_ref[:, :, reach:, :] = jnp.zeros((packed, beams, 8, LANES), jnp.float32)
    own = lax.axis_index("band") * subs
    lane = lax.broadcasted_iota(jnp.int32, (8, LANES), 1)
    row_id = lax.broadcasted_iota(jnp.int32, (QSPAN * packed, LANES), 0)
    lane_id = lax.broadcasted_iota(jnp.int32, (QSPAN * packed, LANES), 1)
    tail_row = lax.broadcasted_iota(jnp.int32, (trial_ranges * packed, LANES), 0)
    tail_lane = lax.broadcasted_iota(jnp.int32, (trial_ranges * packed, LANES), 1)
    for group in range(subs // packed):
        for place in range(packed):
            sub = group * packed + place
            tiled = jnp.concatenate([delay_ref[sub]] * packed, axis=0).astype(jnp.float32).T
            tiled = tiled - (lax.broadcasted_iota(jnp.int32, tiled.shape, 1) // q_count).astype(jnp.float32)
            selector = jnp.concatenate([jnp.where(tiled == jnp.float32(tile * packed), 1.0, 0.0).astype(jnp.bfloat16) for tile in range(tiles)], axis=1)
            copies[sub].wait()
            for beam in range(beams):
                lagged_ref[beam, MAXD1:reach, :] = lax.dot_general(
                    x_ref[sub, beam], selector, (((0,), (0,)), ((), ())), preferred_element_type=jnp.float32
                )
                for start in range(0, reach, 8):
                    total = lagged_ref[beam, start : start + 8, :LANES]
                    for tile in range(1, tiles):
                        at = start + packed * tile
                        total = total + lagged_ref[beam, at : at + 8, tile * LANES : (tile + 1) * LANES]
                    joined_ref[place, beam, start : start + 8, :] = total
        firsts = [[span_ref[target, own + group * packed + place] for place in range(packed)] for target in range(trial_ranges)]
        chooser = []
        for target in range(trial_ranges):
            column = jnp.zeros((per_range, LANES), jnp.int32)
            for place in range(packed):
                column = jnp.where(row_id % packed == place, firsts[target][place] + place * q_count, column)
            chooser.append((lane_id == column + row_id // packed).astype(jnp.float32))
        chooser = jnp.concatenate(chooser, axis=0).astype(jnp.bfloat16)
        tail_column = jnp.zeros((trial_ranges * packed, LANES), jnp.int32)
        for target in range(trial_ranges):
            for place in range(packed):
                tail_column = jnp.where(tail_row == target * packed + place, firsts[target][place] + place * q_count, tail_column)
        tail_chooser = jnp.concatenate([(tail_lane == tail_column + span).astype(jnp.float32) for span in range(QSPAN)], axis=0).astype(jnp.bfloat16)
        for beam in range(beams):
            pieces = []
            for start in list(range(MAXD1, reach, 8)) + list(range(0, MAXD1, 8)):
                total = None
                for turn in range(packed):
                    mixed = None
                    for part in range(packed):
                        there = (part + turn) % packed
                        piece = joined_ref[there, beam, start + part : start + part + 8, :]
                        mixed = piece if mixed is None else jnp.where(lane >= part * q_count, piece, mixed)
                    if turn:
                        mixed = pltpu.roll(mixed, turn * q_count, 1)
                    total = mixed if total is None else total + mixed
                pieces.append(total)
            rows = jnp.concatenate(pieces, axis=0).astype(jnp.bfloat16)
            chosen = lax.dot_general(
                chooser, rows[:block_len], (((1,), (1,)), ((), ())), preferred_element_type=jnp.float32
            ).astype(jnp.bfloat16)
            for target in range(trial_ranges):
                for half in range(halves):
                    at = ((group * beams + beam) * halves + half) * per_range
                    out_ref[target, at : at + per_range, :] = chosen[
                        target * per_range : (target + 1) * per_range, half * LANES : (half + 1) * LANES
                    ]
            tails = lax.dot_general(
                tail_chooser, rows[block_len:], (((1,), (1,)), ((), ())), preferred_element_type=jnp.float32
            )
            step = trial_ranges * packed
            tails = jnp.concatenate([tails[span * step : (span + 1) * step] for span in range(QSPAN)], axis=1)
            for target in range(trial_ranges):
                tail_ref[target, pl.ds((group * beams + beam) * packed, packed), :] = tails[target * packed : (target + 1) * packed]
    main = subs * beams * halves * QSPAN
    for target in range(trial_ranges):
        out_ref[target, main:, :] = tail_ref[target].astype(jnp.bfloat16)


def spread(subs, beams, packed, recv_ref, wide_ref, flat_ref):
    sources, rows, _ = recv_ref.shape
    halves = 2
    blocks = sources * halves
    main = subs * beams * halves * QSPAN
    for source in range(sources):
        flat_ref[source * rows : (source + 1) * rows] = recv_ref[source].astype(jnp.float32)
    flat_ref[sources * rows :] = jnp.zeros((rows, LANES), jnp.float32)
    lane = lax.broadcasted_iota(jnp.int32, (sources, LANES), 1)
    for pair in range(subs * beams):
        sub, beam = pair // beams, pair % beams
        group, inside = sub // packed, sub % packed
        tail_at = main + (group * beams + beam) * packed + inside
        tails = flat_ref[pl.ds(rows + tail_at, sources, stride=rows), :]
        for span in range(QSPAN):
            row = pair * QSPAN + span
            wide_ref[row, blocks:, :] = jnp.zeros((wide_ref.shape[1] - blocks, LANES), jnp.float32)
            for half in range(halves):
                place = (((group * beams + beam) * halves + half) * QSPAN + span) * packed + inside
                piece = flat_ref[pl.ds(place, sources, stride=rows), :]
                if half == halves - 1:
                    turn = (LANES - MAXD1 - span * MAXD1) % LANES
                    moved = pltpu.roll(tails, turn, 1) if turn else tails
                    piece = piece + jnp.where(lane >= LANES - MAXD1, moved, 0.0)
                wide_ref[row, pl.ds(half, sources, stride=halves), :] = piece


def add_trials(subs, beams, first, count, place_ref, wide_ref, sums_ref, out_ref):
    blocks = sums_ref.shape[0] // (beams * count)
    lane = lax.broadcasted_iota(jnp.int32, (8, LANES), 1)

    def one_trial(inside, carry):
        sums = [[None] * (blocks // 8) for _ in range(beams)]
        for sub in range(subs):
            place = place_ref[sub, first + inside]
            row = place >> 20
            coarse = (place >> 7) & 0x1FFF
            fine = place & (LANES - 1)
            keep = lane >= fine
            turn = (LANES - fine) & (LANES - 1)
            for beam in range(beams):
                for part in range(blocks // 8):
                    at = coarse + part * 8
                    near = wide_ref[row + beam * QSPAN, pl.ds(at, 8), :]
                    far = wide_ref[row + beam * QSPAN, pl.ds(at + 1, 8), :]
                    moved = pltpu.roll(jnp.where(keep, near, far), turn, 1)
                    held = sums[beam][part]
                    sums[beam][part] = moved if held is None else held + moved
        for beam in range(beams):
            for part in range(blocks // 8):
                start = part * 8 * beams * count + beam * count + inside
                sums_ref[pl.ds(start, 8, stride=beams * count), :] = sums[beam][part]
        return carry

    lax.fori_loop(0, count, one_trial, 0, unroll=min(count, 8))
    out_ref[...] = sums_ref[...].reshape(out_ref.shape).astype(out_ref.dtype)


def partner(place, step, peers):
    return place ^ step if peers & (peers - 1) == 0 else (place + step) % peers


def first_kernel(subs, beams, packed, bands, step, count, place_ref, recv_ref, wide_ref, out_ref, flat_ref, sums_ref):
    spread(subs, beams, packed, recv_ref, wide_ref, flat_ref)
    band = partner(lax.axis_index("band"), step, bands)
    add_trials(subs, beams, band * count, count, place_ref, wide_ref, sums_ref, out_ref)


def next_kernel(subs, beams, bands, steps, count, place_ref, wide_ref, *refs):
    for step, out_ref in zip(steps, refs):
        band = partner(lax.axis_index("band"), step, bands)
        add_trials(subs, beams, band * count, count, place_ref, wide_ref, refs[-1], out_ref)


def peak_kernel(beams, scale, width_ref, *refs):
    x_refs, (series_ref, peak_ref) = refs[:-2], refs[-2:]
    blocks, rows, _ = x_refs[0].shape
    per_beam = rows // beams
    series = []
    for block in range(blocks):
        total = x_refs[0][block].astype(jnp.float32)
        for x_ref in x_refs[1:]:
            total = total + x_ref[block].astype(jnp.float32)
        series.append((total / scale).astype(jnp.bfloat16))
    for block in range(blocks):
        for beam in range(beams):
            series_ref[beam, :, block * LANES : (block + 1) * LANES] = (
                series[block].astype(jnp.float32)[beam * per_beam : (beam + 1) * per_beam].astype(jnp.bfloat16)
            )
    following = series[1:] + [jnp.zeros_like(series[0])]
    left = jnp.concatenate(
        [jnp.concatenate([here, after], axis=1) for here, after in zip(series, following)], axis=0
    )
    source = lax.broadcasted_iota(jnp.int32, (2 * LANES, LANES), 0)
    place = lax.broadcasted_iota(jnp.int32, (2 * LANES, LANES), 1)
    for slot in range(peak_ref.shape[1]):
        width = width_ref[slot]
        window = ((source >= place) & (source < place + width)).astype(jnp.bfloat16)
        totals = jnp.dot(left, window, preferred_element_type=jnp.float32)
        best = totals[:rows]
        for block in range(1, blocks):
            best = jnp.maximum(best, totals[block * rows : (block + 1) * rows])
        root = jnp.sqrt(jnp.full((1, rows), width, jnp.int32).astype(jnp.float32))
        peaks = jnp.max(best.T, axis=0, keepdims=True) / root
        for beam in range(beams):
            peak_ref[beam, slot : slot + 1, :] = peaks[:, beam * per_beam : (beam + 1) * per_beam]


def local(intensity, fine_delay, span_start, sub_rel, offset, widths):
    beams, channels, block_len = intensity.shape
    subs, q_count, width = fine_delay.shape
    sources = lax.axis_size("trial")
    bands = lax.axis_size("band")
    trials = sub_rel.shape[0]
    halves = block_len // LANES
    packed = LANES // q_count
    blocks = sources * halves
    length = sources * block_len
    main = subs * beams * halves * QSPAN
    rows = round_up(main + subs * beams, 16)
    in_smem = pl.BlockSpec(memory_space=pltpu.SMEM)
    in_vmem = pl.BlockSpec(memory_space=pltpu.VMEM)
    small = pltpu.CompilerParams(vmem_limit_bytes=16 << 20)
    send = pl.pallas_call(
        functools.partial(fine_kernel, sources),
        in_specs=[in_smem, pl.BlockSpec(memory_space=pl.ANY), in_vmem],
        out_specs=in_vmem,
        scratch_shapes=[
            pltpu.VMEM((subs, beams, width, block_len), jnp.bfloat16),
            pltpu.VMEM((beams, block_len + 2 * MAXD1, MAXD1 * q_count), jnp.float32),
            pltpu.VMEM((packed, beams, block_len + MAXD1 + 8, LANES), jnp.float32),
            pltpu.VMEM((sources, rows - main, LANES), jnp.float32),
            pltpu.SemaphoreType.DMA((subs,)),
        ],
        out_shape=jax.ShapeDtypeStruct((sources, rows, LANES), jnp.bfloat16),
        compiler_params=pltpu.CompilerParams(vmem_limit_bytes=61 << 20),
        name="fine_delays",
    )(span_start, intensity, fine_delay)
    own = lax.axis_index("band") * subs
    own_rel = lax.dynamic_slice_in_dim(sub_rel.T, own, subs, 0)
    own_shift = lax.dynamic_slice_in_dim(offset.T, own, subs, 0)
    pair = jnp.arange(subs, dtype=jnp.int32)[:, None] * beams
    places = ((pair * QSPAN + own_rel) << 20) + own_shift
    received = lax.all_to_all(send, "trial", split_axis=0, concat_axis=0, tiled=True)
    stride = round_up(blocks + length // 2 // LANES + 1, 8)
    count = trials // bands
    chunk_shape = (blocks, beams * count, LANES)
    sums_scratch = pltpu.VMEM((blocks * beams * count, LANES), jnp.float32)
    steps = list(range(bands - 1, -1, -1))
    chunks = [jax.ShapeDtypeStruct(chunk_shape, jnp.bfloat16 if step else jnp.float32) for step in steps]
    wide, first = pl.pallas_call(
        functools.partial(first_kernel, subs, beams, packed, bands, steps[0], count),
        in_specs=[in_smem, in_vmem],
        out_specs=[in_vmem, in_vmem],
        scratch_shapes=[pltpu.VMEM(((sources + 1) * rows, LANES), jnp.float32), sums_scratch],
        out_shape=[jax.ShapeDtypeStruct((subs * beams * QSPAN, stride, LANES), jnp.float32), chunks[0]],
        compiler_params=small,
        name="spread_and_add",
    )(places, received)
    rest = pl.pallas_call(
        functools.partial(next_kernel, subs, beams, bands, steps[1:], count),
        in_specs=[in_smem, in_vmem],
        out_specs=[in_vmem] * (bands - 1),
        scratch_shapes=[sums_scratch],
        out_shape=chunks[1:],
        compiler_params=small,
        cost_estimate=pl.CostEstimate(flops=4 << 30, bytes_accessed=12 << 20, transcendentals=0),
        name="add_trials",
    )(places, wide)
    arrived = [rest[-1]]
    for step, sums in zip(steps[:-1], [first] + list(rest[:-1])):
        pairs = [(place, partner(place, step, bands)) for place in range(bands)]
        arrived.append(lax.ppermute(sums, "band", pairs))
    series, peaks = pl.pallas_call(
        functools.partial(peak_kernel, beams, math.sqrt(channels * bands)),
        in_specs=[in_smem] + [in_vmem] * bands,
        out_specs=[in_vmem] * 2,
        out_shape=[
            jax.ShapeDtypeStruct((beams, count, length), jnp.bfloat16),
            jax.ShapeDtypeStruct((beams, widths.shape[0], count), jnp.float32),
        ],
        compiler_params=small,
        name="boxcar_peaks",
    )(widths, *arrived)
    return series, peaks.swapaxes(1, 2)


def solution(mesh):
    return jax.shard_map(
        lambda *arrays: tuple(local(*arrays)),
        mesh=mesh,
        in_specs=(
            P(None, "band", "trial"),
            P("band", None, None),
            P(),
            P("trial", None),
            P("trial", None),
            P(),
        ),
        out_specs=(P(None, ("trial", "band"), None), P(None, ("trial", "band"), None)),
        check_vma=False,
    )
```

```python
import functools
import math

import jax
import jax.numpy as jnp
from jax import lax
from jax.experimental import pallas as pl
from jax.experimental.pallas import tpu as pltpu
from jax.sharding import PartitionSpec as P

QSPAN = 4
MAXD1 = 32
LANES = 128


def round_up(number, step):
    return (number + step - 1) // step * step


def fine_kernel(trial_ranges, span_ref, x_hbm, delay_hbm, *refs):
    (keep_ref, swap_ref, x_ref, delay_ref, turned_ref, lagged_ref, joined_ref, tail_ref, sems) = refs
    subs, beams, width, block_len = x_ref.shape
    q_count = delay_ref.shape[1]
    packed = LANES // q_count
    step = MAXD1 // 2
    tiles = step // packed
    halves = block_len // LANES
    reach = MAXD1 + block_len
    unit = trial_ranges * QSPAN * packed
    per_range = QSPAN * packed
    lead = min(3, subs)
    early = 1
    copies = [
        pltpu.make_async_copy(x_hbm.at[:, pl.ds(sub * width, width), :], x_ref.at[sub], sems.at[sub])
        for sub in range(subs)
    ]
    delay_copies = [
        pltpu.make_async_copy(delay_hbm.at[pl.ds(0, early)], delay_ref.at[pl.ds(0, early)], sems.at[subs]),
        pltpu.make_async_copy(delay_hbm.at[pl.ds(early, subs - early)], delay_ref.at[pl.ds(early, subs - early)], sems.at[subs + 1]),
    ]
    delay_copies[0].start()
    copies[0].start()
    copies[1].start()
    delay_copies[1].start()
    for sub in range(2, lead):
        copies[sub].start()
    for parity in range(turned_ref.shape[0]):
        for beam in range(beams):
            turned_ref[parity, beam, :step, :] = jnp.zeros((step, width), jnp.bfloat16)
            turned_ref[parity, beam, step + block_len :, :] = jnp.zeros((step, width), jnp.bfloat16)
    for parity in range(lagged_ref.shape[0]):
        for beam in range(beams):
            lagged_ref[parity, beam, :step, :] = jnp.zeros((step, step * q_count), jnp.float32)
            lagged_ref[parity, beam, reach:, :] = jnp.zeros((step, step * q_count), jnp.float32)
    joined_ref[:, :, reach:, :] = jnp.zeros((subs, beams, 8, LANES), jnp.float32)
    lane_part = (lax.broadcasted_iota(jnp.int32, (width, LANES), 1) // q_count).astype(jnp.float32)
    own = lax.axis_index("band") * subs
    me = lax.axis_index("trial")
    lane = lax.broadcasted_iota(jnp.int32, (8, LANES), 1)
    row_id = lax.broadcasted_iota(jnp.int32, (QSPAN * packed, LANES), 0)
    lane_id = lax.broadcasted_iota(jnp.int32, (QSPAN * packed, LANES), 1)
    tail_row = lax.broadcasted_iota(jnp.int32, (trial_ranges * packed, LANES), 0)
    tail_lane = lax.broadcasted_iota(jnp.int32, (trial_ranges * packed, LANES), 1)
    def one_sub(sub):
        if sub == 0:
            delay_copies[0].wait()
        if sub == early:
            delay_copies[1].wait()
        tiled = jnp.concatenate([delay_ref[sub]] * packed, axis=0).astype(jnp.float32).T - lane_part
        selector = jnp.concatenate(
            [
                jnp.concatenate(
                    [
                        jnp.where(tiled == jnp.float32(half * step + tile * packed), 1.0, 0.0).astype(jnp.bfloat16)
                        for tile in range(tiles)
                    ],
                    axis=1,
                )
                for half in range(2)
            ],
            axis=0,
        )
        copies[sub].wait()
        if sub + lead < subs:
            copies[sub + lead].start()
        side, other = sub % turned_ref.shape[0], sub % lagged_ref.shape[0]
        left = []
        for beam in range(beams):
            turned_ref[side, beam, step : step + block_len, :] = x_ref[sub, beam].T
            left.append(
                jnp.concatenate(
                    [turned_ref[side, beam, : step + block_len, :], turned_ref[side, beam, step : 2 * step + block_len, :]],
                    axis=1,
                )
            )
        both = jnp.dot(jnp.concatenate(left, axis=0), selector, preferred_element_type=jnp.float32)
        for beam in range(beams):
            lagged_ref[other, beam, step:reach, :] = both[beam * (step + block_len) : (beam + 1) * (step + block_len)]
        for beam in range(beams):
            for start in range(0, reach, 8):
                total = lagged_ref[other, beam, start : start + 8, :LANES]
                for tile in range(1, tiles):
                    at = start + packed * tile
                    total = total + lagged_ref[other, beam, at : at + 8, tile * LANES : (tile + 1) * LANES]
                joined_ref[sub, beam, start : start + 8, :] = total

    def choose(group):
        firsts = [[span_ref[me ^ target, own + group * packed + place] for place in range(packed)] for target in range(trial_ranges)]
        chooser = []
        for target in range(trial_ranges):
            column = jnp.zeros((per_range, LANES), jnp.int32)
            for place in range(packed):
                column = jnp.where(row_id % packed == place, firsts[target][place] + place * q_count, column)
            chooser.append((lane_id == column + row_id // packed).astype(jnp.float32))
        chooser = jnp.concatenate(chooser, axis=0).astype(jnp.bfloat16)
        tail_column = jnp.zeros((trial_ranges * packed, LANES), jnp.int32)
        for target in range(trial_ranges):
            for place in range(packed):
                tail_column = jnp.where(tail_row == target * packed + place, firsts[target][place] + place * q_count, tail_column)
        tail_chooser = jnp.concatenate([(tail_lane == tail_column + span).astype(jnp.float32) for span in range(QSPAN)], axis=0).astype(jnp.bfloat16)
        for beam in range(beams):
            pieces = []
            for start in list(range(MAXD1, reach, 8)) + list(range(0, MAXD1, 8)):
                total = None
                for turn in range(packed):
                    mixed = None
                    for part in range(packed):
                        there = (part + turn) % packed
                        piece = joined_ref[group * packed + there, beam, start + part : start + part + 8, :]
                        mixed = piece if mixed is None else jnp.where(lane >= part * q_count, piece, mixed)
                    if turn:
                        mixed = pltpu.roll(mixed, turn * q_count, 1)
                    total = mixed if total is None else total + mixed
                pieces.append(total)
            rows = jnp.concatenate(pieces, axis=0).astype(jnp.bfloat16)
            chosen = lax.dot_general(
                chooser, rows[:block_len], (((1,), (1,)), ((), ())), preferred_element_type=jnp.float32
            ).astype(jnp.bfloat16)
            for target in range(trial_ranges):
                for half in range(halves):
                    at = ((group * beams + beam) * halves + half) * per_range
                    (keep_ref, swap_ref)[target % 2][target // 2, at : at + per_range, :] = chosen[
                        target * per_range : (target + 1) * per_range, half * LANES : (half + 1) * LANES
                    ]
            tails = lax.dot_general(
                tail_chooser, rows[block_len:], (((1,), (1,)), ((), ())), preferred_element_type=jnp.float32
            )
            units = trial_ranges * packed
            tails = jnp.concatenate([tails[span * units : (span + 1) * units] for span in range(QSPAN)], axis=1)
            for target in range(trial_ranges):
                tail_ref[target, pl.ds((group * beams + beam) * packed, packed), :] = tails[target * packed : (target + 1) * packed]

    for sub in range(subs):
        one_sub(sub)
        if sub and sub % packed == 0:
            choose(sub // packed - 1)
    choose(subs // packed - 1)
    main = subs * beams * halves * QSPAN
    for target in range(trial_ranges):
        (keep_ref, swap_ref)[target % 2][target // 2, main:, :] = tail_ref[target].astype(jnp.bfloat16)


def pair_kernel(keep_ref, swap_ref, *out_refs):
    for place, out_ref in enumerate(out_refs):
        out_ref[0] = keep_ref[place]
        out_ref[1] = swap_ref[place]


def spread(subs, beams, packed, recv_refs, wide_ref, flat_ref):
    _, rows, _ = recv_refs[0].shape
    sources = 2 * len(recv_refs)
    halves = 2
    blocks = sources * halves
    main = subs * beams * halves * QSPAN
    me = lax.axis_index("trial")
    for step in range(sources):
        at = pl.multiple_of((me ^ step) * rows, 16)
        flat_ref[pl.ds(at, rows), :] = recv_refs[step // 2][step % 2].astype(jnp.float32)
    flat_ref[sources * rows :] = jnp.zeros((rows, LANES), jnp.float32)
    lane = lax.broadcasted_iota(jnp.int32, (sources, LANES), 1)
    for pair in range(subs * beams):
        sub, beam = pair // beams, pair % beams
        group, inside = sub // packed, sub % packed
        tail_at = main + (group * beams + beam) * packed + inside
        tails = flat_ref[pl.ds(rows + tail_at, sources, stride=rows), :]
        for span in range(QSPAN):
            row = pair * QSPAN + span
            wide_ref[row, blocks:, :] = jnp.zeros((wide_ref.shape[1] - blocks, LANES), jnp.float32)
            for half in range(halves):
                place = (((group * beams + beam) * halves + half) * QSPAN + span) * packed + inside
                piece = flat_ref[pl.ds(place, sources, stride=rows), :]
                if half == halves - 1:
                    turn = (LANES - MAXD1 - span * MAXD1) % LANES
                    moved = pltpu.roll(tails, turn, 1) if turn else tails
                    piece = piece + jnp.where(lane >= LANES - MAXD1, moved, 0.0)
                wide_ref[row, pl.ds(half, sources, stride=halves), :] = piece


def add_trials(subs, beams, first, count, place_ref, wide_ref, sums_ref, out_ref):
    blocks = sums_ref.shape[0] // (beams * count)
    lane = lax.broadcasted_iota(jnp.int32, (8, LANES), 1)

    def one_trial(inside, carry):
        sums = [[None] * (blocks // 8) for _ in range(beams)]
        for sub in range(subs):
            place = place_ref[sub, first + inside]
            row = place >> 20
            coarse = (place >> 7) & 0x1FFF
            fine = place & (LANES - 1)
            keep = lane >= fine
            turn = (LANES - fine) & (LANES - 1)
            for beam in range(beams):
                for part in range(blocks // 8):
                    at = coarse + part * 8
                    near = wide_ref[row + beam * QSPAN, pl.ds(at, 8), :]
                    far = wide_ref[row + beam * QSPAN, pl.ds(at + 1, 8), :]
                    moved = pltpu.roll(jnp.where(keep, near, far), turn, 1)
                    held = sums[beam][part]
                    sums[beam][part] = moved if held is None else held + moved
        for beam in range(beams):
            for part in range(blocks // 8):
                start = part * 8 * beams * count + beam * count + inside
                sums_ref[pl.ds(start, 8, stride=beams * count), :] = sums[beam][part]
        return carry

    lax.fori_loop(0, count, one_trial, 0, unroll=min(count, 8))
    out_ref[...] = sums_ref[...].reshape(out_ref.shape).astype(out_ref.dtype)


def partner(place, step, peers):
    return place ^ step if peers & (peers - 1) == 0 else (place + step) % peers


def first_kernel(subs, beams, packed, bands, step, count, place_ref, *refs):
    wide_ref, out_ref, flat_ref, sums_ref = refs[-4:]
    spread(subs, beams, packed, refs[:-4], wide_ref, flat_ref)
    band = partner(lax.axis_index("band"), step, bands)
    add_trials(subs, beams, band * count, count, place_ref, wide_ref, sums_ref, out_ref)


def next_kernel(subs, beams, bands, steps, count, place_ref, wide_ref, *refs):
    for step, out_ref in zip(steps, refs):
        band = partner(lax.axis_index("band"), step, bands)
        add_trials(subs, beams, band * count, count, place_ref, wide_ref, refs[-1], out_ref)


def peak_kernel(beams, scale, width_ref, *refs):
    x_refs, (series_ref, peak_ref) = refs[:-2], refs[-2:]
    blocks, rows, _ = x_refs[0].shape
    per_beam = rows // beams
    series = []
    for block in range(blocks):
        total = x_refs[0][block].astype(jnp.float32)
        for x_ref in x_refs[1:]:
            total = total + x_ref[block].astype(jnp.float32)
        series.append((total / scale).astype(jnp.bfloat16))
    for block in range(blocks):
        for beam in range(beams):
            series_ref[beam, :, block * LANES : (block + 1) * LANES] = (
                series[block].astype(jnp.float32)[beam * per_beam : (beam + 1) * per_beam].astype(jnp.bfloat16)
            )
    following = series[1:] + [jnp.zeros_like(series[0])]
    left = jnp.concatenate(
        [jnp.concatenate([here, after], axis=1) for here, after in zip(series, following)], axis=0
    )
    source = lax.broadcasted_iota(jnp.int32, (2 * LANES, LANES), 0)
    place = lax.broadcasted_iota(jnp.int32, (2 * LANES, LANES), 1)
    for slot in range(peak_ref.shape[1]):
        width = width_ref[slot]
        window = ((source >= place) & (source < place + width)).astype(jnp.bfloat16)
        totals = jnp.dot(left, window, preferred_element_type=jnp.float32)
        best = totals[:rows]
        for block in range(1, blocks):
            best = jnp.maximum(best, totals[block * rows : (block + 1) * rows])
        root = jnp.sqrt(jnp.full((1, rows), width, jnp.int32).astype(jnp.float32))
        peaks = jnp.max(best.T, axis=0, keepdims=True) / root
        for beam in range(beams):
            peak_ref[beam, slot : slot + 1, :] = peaks[:, beam * per_beam : (beam + 1) * per_beam]


def local(intensity, fine_delay, span_start, sub_rel, offset, widths):
    beams, channels, block_len = intensity.shape
    subs, q_count, width = fine_delay.shape
    sources = lax.axis_size("trial")
    bands = lax.axis_size("band")
    trials = sub_rel.shape[0]
    halves = block_len // LANES
    packed = LANES // q_count
    blocks = sources * halves
    length = sources * block_len
    main = subs * beams * halves * QSPAN
    rows = round_up(main + subs * beams, 16)
    in_smem = pl.BlockSpec(memory_space=pltpu.SMEM)
    in_vmem = pl.BlockSpec(memory_space=pltpu.VMEM)
    small = pltpu.CompilerParams(vmem_limit_bytes=16 << 20)
    chips = sources // 2
    keep, swap = pl.pallas_call(
        functools.partial(fine_kernel, sources),
        in_specs=[in_smem] + [pl.BlockSpec(memory_space=pl.ANY)] * 2,
        out_specs=[in_vmem] * 2,
        scratch_shapes=[
            pltpu.VMEM((subs, beams, width, block_len), jnp.bfloat16),
            pltpu.VMEM((subs, q_count, width), jnp.int32),
            pltpu.VMEM((1, beams, block_len + MAXD1, width), jnp.bfloat16),
            pltpu.VMEM((1, beams, block_len + MAXD1 + MAXD1 // 2, MAXD1 // 2 * q_count), jnp.float32),
            pltpu.VMEM((subs, beams, block_len + MAXD1 + 8, LANES), jnp.float32),
            pltpu.VMEM((sources, rows - main, LANES), jnp.float32),
            pltpu.SemaphoreType.DMA((subs + 2,)),
        ],
        out_shape=[pltpu.VMEM((chips, rows, LANES), jnp.bfloat16)] * 2,
        compiler_params=pltpu.CompilerParams(vmem_limit_bytes=61 << 20),
        name="fine_delays",
    )(span_start, intensity, fine_delay)
    own = lax.axis_index("band") * subs
    own_rel = lax.dynamic_slice_in_dim(sub_rel.T, own, subs, 0)
    own_shift = lax.dynamic_slice_in_dim(offset.T, own, subs, 0)
    pair = jnp.arange(subs, dtype=jnp.int32)[:, None] * beams
    places = ((pair * QSPAN + own_rel) << 20) + own_shift

    def crossed(array, step):
        return lax.ppermute(array, "trial", [(place, place ^ step) for place in range(sources)])

    pairs = pl.pallas_call(
        pair_kernel,
        in_specs=[in_vmem] * 2,
        out_specs=[in_vmem] * chips,
        out_shape=[jax.ShapeDtypeStruct((2, rows, LANES), jnp.bfloat16)] * chips,
        compiler_params=small,
        name="pair_rows",
    )(keep, crossed(swap, 1))
    received = [pairs[0]] + [crossed(pairs[step], 2 * step) for step in range(1, chips)]
    stride = round_up(blocks + length // 2 // LANES + 1, 8)
    count = trials // bands
    chunk_shape = (blocks, beams * count, LANES)
    sums_scratch = pltpu.VMEM((blocks * beams * count, LANES), jnp.float32)
    steps = list(range(bands - 1, -1, -1))
    chunks = [jax.ShapeDtypeStruct(chunk_shape, jnp.bfloat16 if step else jnp.float32) for step in steps]
    wide, first = pl.pallas_call(
        functools.partial(first_kernel, subs, beams, packed, bands, steps[0], count),
        in_specs=[in_smem] + [in_vmem] * chips,
        out_specs=[in_vmem, in_vmem],
        scratch_shapes=[pltpu.VMEM(((sources + 1) * rows, LANES), jnp.float32), sums_scratch],
        out_shape=[jax.ShapeDtypeStruct((subs * beams * QSPAN, stride, LANES), jnp.float32), chunks[0]],
        compiler_params=small,
        name="spread_and_add",
    )(places, *received)
    rest = pl.pallas_call(
        functools.partial(next_kernel, subs, beams, bands, steps[1:], count),
        in_specs=[in_smem, in_vmem],
        out_specs=[in_vmem] * (bands - 1),
        scratch_shapes=[sums_scratch],
        out_shape=chunks[1:],
        compiler_params=small,
        cost_estimate=pl.CostEstimate(flops=4 << 30, bytes_accessed=12 << 20, transcendentals=0),
        name="add_trials",
    )(places, wide)
    arrived = []
    for step, sums in zip(steps[:-1], [first] + list(rest[:-1])):
        pairs = [(place, partner(place, step, bands)) for place in range(bands)]
        arrived.append(lax.ppermute(sums, "band", pairs))
    arrived = [rest[-1] + arrived[0].astype(jnp.float32)] + arrived[1:]
    series, peaks = pl.pallas_call(
        functools.partial(peak_kernel, beams, math.sqrt(channels * bands)),
        in_specs=[in_smem] + [in_vmem] * len(arrived),
        out_specs=[in_vmem] * 2,
        out_shape=[
            jax.ShapeDtypeStruct((beams, count, length), jnp.bfloat16),
            jax.ShapeDtypeStruct((beams, widths.shape[0], count), jnp.float32),
        ],
        compiler_params=small,
        name="boxcar_peaks",
    )(widths, *arrived)
    return series, peaks.swapaxes(1, 2)


def solution(mesh):
    return jax.shard_map(
        lambda *arrays: tuple(local(*arrays)),
        mesh=mesh,
        in_specs=(
            P(None, "band", "trial"),
            P("band", None, None),
            P(),
            P("trial", None),
            P("trial", None),
            P(),
        ),
        out_specs=(P(None, ("trial", "band"), None), P(None, ("trial", "band"), None)),
        check_vma=False,
    )
```

```python
import functools
import math

import jax
import jax.numpy as jnp
from jax import lax
from jax.experimental import pallas as pl
from jax.experimental.pallas import tpu as pltpu
from jax.sharding import PartitionSpec as P

QSPAN = 4
MAXD1 = 32
LANES = 128


def round_up(number, step):
    return (number + step - 1) // step * step


def fine_kernel(trial_ranges, span_any, x_hbm, delay_hbm, *refs):
    (keep_ref, swap_ref, x_ref, delay_ref, turned_ref, lagged_ref, joined_ref, tail_ref, span_ref, sems) = refs
    subs, beams, width, block_len = x_ref.shape
    q_count = delay_ref.shape[1]
    packed = LANES // q_count
    step = MAXD1 // 2
    tiles = step // packed
    halves = block_len // LANES
    reach = MAXD1 + block_len
    unit = trial_ranges * QSPAN * packed
    per_range = QSPAN * packed
    lead = min(3, subs)
    early = 1
    copies = [
        pltpu.make_async_copy(x_hbm.at[:, pl.ds(sub * width, width), :], x_ref.at[sub], sems.at[sub])
        for sub in range(subs)
    ]
    delay_copies = [
        pltpu.make_async_copy(delay_hbm.at[pl.ds(0, early)], delay_ref.at[pl.ds(0, early)], sems.at[subs]),
        pltpu.make_async_copy(delay_hbm.at[pl.ds(early, subs - early)], delay_ref.at[pl.ds(early, subs - early)], sems.at[subs + 1]),
    ]
    span_copy = pltpu.make_async_copy(span_any, span_ref, sems.at[subs + 2])
    delay_copies[0].start()
    copies[0].start()
    span_copy.start()
    copies[1].start()
    delay_copies[1].start()
    for sub in range(2, lead):
        copies[sub].start()
    for parity in range(turned_ref.shape[0]):
        for beam in range(beams):
            turned_ref[parity, beam, :step, :] = jnp.zeros((step, width), jnp.bfloat16)
            turned_ref[parity, beam, step + block_len :, :] = jnp.zeros((step, width), jnp.bfloat16)
    for parity in range(lagged_ref.shape[0]):
        for beam in range(beams):
            lagged_ref[parity, beam, :step, :] = jnp.zeros((step, step * q_count), jnp.float32)
            lagged_ref[parity, beam, reach:, :] = jnp.zeros((step, step * q_count), jnp.float32)
    joined_ref[:, :, reach:, :] = jnp.zeros((subs, beams, 8, LANES), jnp.float32)
    lane_part = (lax.broadcasted_iota(jnp.int32, (width, LANES), 1) // q_count).astype(jnp.float32)
    own = lax.axis_index("band") * subs
    me = lax.axis_index("trial")
    lane = lax.broadcasted_iota(jnp.int32, (8, LANES), 1)
    row_id = lax.broadcasted_iota(jnp.int32, (QSPAN * packed, LANES), 0)
    lane_id = lax.broadcasted_iota(jnp.int32, (QSPAN * packed, LANES), 1)
    tail_row = lax.broadcasted_iota(jnp.int32, (trial_ranges * packed, LANES), 0)
    tail_lane = lax.broadcasted_iota(jnp.int32, (trial_ranges * packed, LANES), 1)
    def one_sub(sub):
        if sub == 0:
            delay_copies[0].wait()
        if sub == early:
            delay_copies[1].wait()
        tiled = jnp.concatenate([delay_ref[sub]] * packed, axis=0).astype(jnp.float32).T - lane_part
        selector = jnp.concatenate(
            [
                jnp.concatenate(
                    [
                        jnp.where(tiled == jnp.float32(half * step + tile * packed), 1.0, 0.0).astype(jnp.bfloat16)
                        for tile in range(tiles)
                    ],
                    axis=1,
                )
                for half in range(2)
            ],
            axis=0,
        )
        copies[sub].wait()
        if sub + lead < subs:
            copies[sub + lead].start()
        side, other = sub % turned_ref.shape[0], sub % lagged_ref.shape[0]
        left = []
        for beam in range(beams):
            turned_ref[side, beam, step : step + block_len, :] = x_ref[sub, beam].T
            left.append(
                jnp.concatenate(
                    [turned_ref[side, beam, : step + block_len, :], turned_ref[side, beam, step : 2 * step + block_len, :]],
                    axis=1,
                )
            )
        both = jnp.dot(jnp.concatenate(left, axis=0), selector, preferred_element_type=jnp.float32)
        for beam in range(beams):
            lagged_ref[other, beam, step:reach, :] = both[beam * (step + block_len) : (beam + 1) * (step + block_len)]
        for beam in range(beams):
            for start in range(0, reach, 8):
                total = lagged_ref[other, beam, start : start + 8, :LANES]
                for tile in range(1, tiles):
                    at = start + packed * tile
                    total = total + lagged_ref[other, beam, at : at + 8, tile * LANES : (tile + 1) * LANES]
                joined_ref[sub, beam, start : start + 8, :] = total

    def choose(group):
        if group == 0:
            span_copy.wait()
        firsts = [[span_ref[me ^ target, own + group * packed + place] for place in range(packed)] for target in range(trial_ranges)]
        chooser = []
        for target in range(trial_ranges):
            column = jnp.zeros((per_range, LANES), jnp.int32)
            for place in range(packed):
                column = jnp.where(row_id % packed == place, firsts[target][place] + place * q_count, column)
            chooser.append((lane_id == column + row_id // packed).astype(jnp.float32))
        chooser = jnp.concatenate(chooser, axis=0).astype(jnp.bfloat16)
        tail_column = jnp.zeros((trial_ranges * packed, LANES), jnp.int32)
        for target in range(trial_ranges):
            for place in range(packed):
                tail_column = jnp.where(tail_row == target * packed + place, firsts[target][place] + place * q_count, tail_column)
        tail_chooser = jnp.concatenate([(tail_lane == tail_column + span).astype(jnp.float32) for span in range(QSPAN)], axis=0).astype(jnp.bfloat16)
        for beam in range(beams):
            pieces = []
            for start in list(range(MAXD1, reach, 8)) + list(range(0, MAXD1, 8)):
                total = None
                for turn in range(packed):
                    mixed = None
                    for part in range(packed):
                        there = (part + turn) % packed
                        piece = joined_ref[group * packed + there, beam, start + part : start + part + 8, :]
                        mixed = piece if mixed is None else jnp.where(lane >= part * q_count, piece, mixed)
                    if turn:
                        mixed = pltpu.roll(mixed, turn * q_count, 1)
                    total = mixed if total is None else total + mixed
                pieces.append(total)
            rows = jnp.concatenate(pieces, axis=0).astype(jnp.bfloat16)
            chosen = lax.dot_general(
                chooser, rows[:block_len], (((1,), (1,)), ((), ())), preferred_element_type=jnp.float32
            ).astype(jnp.bfloat16)
            for target in range(trial_ranges):
                for half in range(halves):
                    at = ((group * beams + beam) * halves + half) * per_range
                    (keep_ref, swap_ref)[target % 2][target // 2, at : at + per_range, :] = chosen[
                        target * per_range : (target + 1) * per_range, half * LANES : (half + 1) * LANES
                    ]
            tails = lax.dot_general(
                tail_chooser, rows[block_len:], (((1,), (1,)), ((), ())), preferred_element_type=jnp.float32
            )
            units = trial_ranges * packed
            tails = jnp.concatenate([tails[span * units : (span + 1) * units] for span in range(QSPAN)], axis=1)
            for target in range(trial_ranges):
                tail_ref[target, pl.ds((group * beams + beam) * packed, packed), :] = tails[target * packed : (target + 1) * packed]

    for sub in range(subs):
        one_sub(sub)
        if sub and sub % packed == 0:
            choose(sub // packed - 1)
    choose(subs // packed - 1)
    main = subs * beams * halves * QSPAN
    for target in range(trial_ranges):
        (keep_ref, swap_ref)[target % 2][target // 2, main:, :] = tail_ref[target].astype(jnp.bfloat16)


def pair_kernel(keep_ref, swap_ref, *out_refs):
    for place, out_ref in enumerate(out_refs):
        out_ref[0] = keep_ref[place]
        out_ref[1] = swap_ref[place]


def spread(subs, beams, packed, recv_refs, wide_ref, flat_ref):
    _, rows, _ = recv_refs[0].shape
    sources = 2 * len(recv_refs)
    halves = 2
    blocks = sources * halves
    main = subs * beams * halves * QSPAN
    me = lax.axis_index("trial")
    for step in range(sources):
        at = pl.multiple_of((me ^ step) * rows, 16)
        flat_ref[pl.ds(at, rows), :] = recv_refs[-1 - step // 2][step % 2].astype(jnp.float32)
    flat_ref[sources * rows :] = jnp.zeros((rows, LANES), jnp.float32)
    lane = lax.broadcasted_iota(jnp.int32, (sources, LANES), 1)
    for pair in range(subs * beams):
        sub, beam = pair // beams, pair % beams
        group, inside = sub // packed, sub % packed
        tail_at = main + (group * beams + beam) * packed + inside
        tails = flat_ref[pl.ds(rows + tail_at, sources, stride=rows), :]
        for span in range(QSPAN):
            row = pair * QSPAN + span
            wide_ref[row, blocks:, :] = jnp.zeros((wide_ref.shape[1] - blocks, LANES), jnp.float32)
            for half in range(halves):
                place = (((group * beams + beam) * halves + half) * QSPAN + span) * packed + inside
                piece = flat_ref[pl.ds(place, sources, stride=rows), :]
                if half == halves - 1:
                    turn = (LANES - MAXD1 - span * MAXD1) % LANES
                    moved = pltpu.roll(tails, turn, 1) if turn else tails
                    piece = piece + jnp.where(lane >= LANES - MAXD1, moved, 0.0)
                wide_ref[row, pl.ds(half, sources, stride=halves), :] = piece


def add_trials(subs, beams, first, count, place_ref, wide_ref, sums_ref, out_ref):
    blocks = sums_ref.shape[0] // (beams * count)
    lane = lax.broadcasted_iota(jnp.int32, (8, LANES), 1)

    def one_trial(inside, carry):
        sums = [[None] * (blocks // 8) for _ in range(beams)]
        for sub in range(subs):
            place = place_ref[sub, first + inside]
            row = place >> 20
            coarse = (place >> 7) & 0x1FFF
            fine = place & (LANES - 1)
            keep = lane >= fine
            turn = (LANES - fine) & (LANES - 1)
            for beam in range(beams):
                for part in range(blocks // 8):
                    at = coarse + part * 8
                    near = wide_ref[row + beam * QSPAN, pl.ds(at, 8), :]
                    far = wide_ref[row + beam * QSPAN, pl.ds(at + 1, 8), :]
                    moved = pltpu.roll(jnp.where(keep, near, far), turn, 1)
                    held = sums[beam][part]
                    sums[beam][part] = moved if held is None else held + moved
        for beam in range(beams):
            for part in range(blocks // 8):
                start = part * 8 * beams * count + beam * count + inside
                sums_ref[pl.ds(start, 8, stride=beams * count), :] = sums[beam][part]
        return carry

    lax.fori_loop(0, count, one_trial, 0, unroll=min(count, 8))
    out_ref[...] = sums_ref[...].reshape(out_ref.shape).astype(out_ref.dtype)


def partner(place, step, peers):
    return place ^ step if peers & (peers - 1) == 0 else (place + step) % peers


def first_kernel(subs, beams, packed, bands, step, count, place_any, *refs):
    wide_ref, out_ref, flat_ref, sums_ref, place_ref, sem = refs[-6:]
    place_copy = pltpu.make_async_copy(place_any, place_ref, sem)
    place_copy.start()
    spread(subs, beams, packed, refs[:-6], wide_ref, flat_ref)
    place_copy.wait()
    band = partner(lax.axis_index("band"), step, bands)
    add_trials(subs, beams, band * count, count, place_ref, wide_ref, sums_ref, out_ref)


def next_kernel(subs, beams, bands, steps, count, place_ref, wide_ref, *refs):
    for step, out_ref in zip(steps, refs):
        band = partner(lax.axis_index("band"), step, bands)
        add_trials(subs, beams, band * count, count, place_ref, wide_ref, refs[-1], out_ref)


def peak_kernel(beams, scale, width_any, *refs):
    x_refs, (series_ref, peak_ref, width_ref, sem) = refs[:-4], refs[-4:]
    width_copy = pltpu.make_async_copy(width_any, width_ref, sem)
    width_copy.start()
    blocks, rows, _ = x_refs[0].shape
    per_beam = rows // beams
    series = []
    for block in range(blocks):
        total = x_refs[0][block].astype(jnp.float32)
        for x_ref in x_refs[1:]:
            total = total + x_ref[block].astype(jnp.float32)
        series.append((total / scale).astype(jnp.bfloat16))
    for block in range(blocks):
        for beam in range(beams):
            series_ref[beam, :, block * LANES : (block + 1) * LANES] = (
                series[block].astype(jnp.float32)[beam * per_beam : (beam + 1) * per_beam].astype(jnp.bfloat16)
            )
    following = series[1:] + [jnp.zeros_like(series[0])]
    left = jnp.concatenate(
        [jnp.concatenate([here, after], axis=1) for here, after in zip(series, following)], axis=0
    )
    width_copy.wait()
    source = lax.broadcasted_iota(jnp.int32, (2 * LANES, LANES), 0)
    place = lax.broadcasted_iota(jnp.int32, (2 * LANES, LANES), 1)
    for slot in range(peak_ref.shape[1]):
        width = width_ref[slot]
        window = ((source >= place) & (source < place + width)).astype(jnp.bfloat16)
        totals = jnp.dot(left, window, preferred_element_type=jnp.float32)
        best = totals[:rows]
        for block in range(1, blocks):
            best = jnp.maximum(best, totals[block * rows : (block + 1) * rows])
        root = jnp.sqrt(jnp.full((1, rows), width, jnp.int32).astype(jnp.float32))
        peaks = jnp.max(best.T, axis=0, keepdims=True) / root
        for beam in range(beams):
            peak_ref[beam, slot : slot + 1, :] = peaks[:, beam * per_beam : (beam + 1) * per_beam]


def local(intensity, fine_delay, span_start, sub_rel, offset, widths):
    beams, channels, block_len = intensity.shape
    subs, q_count, width = fine_delay.shape
    sources = lax.axis_size("trial")
    bands = lax.axis_size("band")
    trials = sub_rel.shape[0]
    halves = block_len // LANES
    packed = LANES // q_count
    blocks = sources * halves
    length = sources * block_len
    main = subs * beams * halves * QSPAN
    rows = round_up(main + subs * beams, 16)
    in_smem = pl.BlockSpec(memory_space=pltpu.SMEM)
    in_vmem = pl.BlockSpec(memory_space=pltpu.VMEM)
    small = pltpu.CompilerParams(vmem_limit_bytes=16 << 20)
    chips = sources // 2
    keep, swap = pl.pallas_call(
        functools.partial(fine_kernel, sources),
        in_specs=[pl.BlockSpec(memory_space=pl.ANY)] * 3,
        out_specs=[in_vmem] * 2,
        scratch_shapes=[
            pltpu.VMEM((subs, beams, width, block_len), jnp.bfloat16),
            pltpu.VMEM((subs, q_count, width), jnp.int32),
            pltpu.VMEM((1, beams, block_len + MAXD1, width), jnp.bfloat16),
            pltpu.VMEM((1, beams, block_len + MAXD1 + MAXD1 // 2, MAXD1 // 2 * q_count), jnp.float32),
            pltpu.VMEM((subs, beams, block_len + MAXD1 + 8, LANES), jnp.float32),
            pltpu.VMEM((sources, rows - main, LANES), jnp.float32),
            pltpu.SMEM(span_start.shape, jnp.int32),
            pltpu.SemaphoreType.DMA((subs + 3,)),
        ],
        out_shape=[pltpu.VMEM((chips, rows, LANES), jnp.bfloat16)] * 2,
        compiler_params=pltpu.CompilerParams(vmem_limit_bytes=61 << 20),
        name="fine_delays",
    )(span_start, intensity, fine_delay)
    own = lax.axis_index("band") * subs
    own_rel = lax.dynamic_slice_in_dim(sub_rel.T, own, subs, 0)
    own_shift = lax.dynamic_slice_in_dim(offset.T, own, subs, 0)
    pair = jnp.arange(subs, dtype=jnp.int32)[:, None] * beams
    places = ((pair * QSPAN + own_rel) << 20) + own_shift

    def crossed(array, step):
        return lax.ppermute(array, "trial", [(place, place ^ step) for place in range(sources)])

    pairs = pl.pallas_call(
        pair_kernel,
        in_specs=[in_vmem] * 2,
        out_specs=[in_vmem] * chips,
        out_shape=[jax.ShapeDtypeStruct((2, rows, LANES), jnp.bfloat16)] * chips,
        compiler_params=small,
        name="pair_rows",
    )(keep, crossed(swap, 1))
    received = [crossed(pairs[step], 2 * step) for step in range(chips - 1, 0, -1)] + [pairs[0]]
    stride = round_up(blocks + length // 2 // LANES + 1, 8)
    count = trials // bands
    chunk_shape = (blocks, beams * count, LANES)
    sums_scratch = pltpu.VMEM((blocks * beams * count, LANES), jnp.float32)
    steps = list(range(bands - 1, -1, -1))
    chunks = [jax.ShapeDtypeStruct(chunk_shape, jnp.bfloat16 if step else jnp.float32) for step in steps]
    wide, first = pl.pallas_call(
        functools.partial(first_kernel, subs, beams, packed, bands, steps[0], count),
        in_specs=[pl.BlockSpec(memory_space=pl.ANY)] + [in_vmem] * chips,
        out_specs=[in_vmem, in_vmem],
        scratch_shapes=[
            pltpu.VMEM(((sources + 1) * rows, LANES), jnp.float32),
            sums_scratch,
            pltpu.SMEM(places.shape, jnp.int32),
            pltpu.SemaphoreType.DMA,
        ],
        out_shape=[jax.ShapeDtypeStruct((subs * beams * QSPAN, stride, LANES), jnp.float32), chunks[0]],
        compiler_params=small,
        name="spread_and_add",
    )(places, *received)
    rest = pl.pallas_call(
        functools.partial(next_kernel, subs, beams, bands, steps[1:], count),
        in_specs=[in_smem, in_vmem],
        out_specs=[in_vmem] * (bands - 1),
        scratch_shapes=[sums_scratch],
        out_shape=chunks[1:],
        compiler_params=small,
        cost_estimate=pl.CostEstimate(flops=4 << 30, bytes_accessed=12 << 20, transcendentals=0),
        name="add_trials",
    )(places, wide)
    arrived = []
    for step, sums in zip(steps[:-1], [first] + list(rest[:-1])):
        pairs = [(place, partner(place, step, bands)) for place in range(bands)]
        arrived.append(lax.ppermute(sums, "band", pairs))
    arrived = [rest[-1] + arrived[0].astype(jnp.float32)] + arrived[1:]
    series, peaks = pl.pallas_call(
        functools.partial(peak_kernel, beams, math.sqrt(channels * bands)),
        in_specs=[pl.BlockSpec(memory_space=pl.ANY)] + [in_vmem] * len(arrived),
        out_specs=[in_vmem] * 2,
        scratch_shapes=[pltpu.SMEM(widths.shape, jnp.int32), pltpu.SemaphoreType.DMA],
        out_shape=[
            jax.ShapeDtypeStruct((beams, count, length), jnp.bfloat16),
            jax.ShapeDtypeStruct((beams, widths.shape[0], count), jnp.float32),
        ],
        compiler_params=small,
        name="boxcar_peaks",
    )(widths, *arrived)
    return series, peaks.swapaxes(1, 2)


def solution(mesh):
    return jax.shard_map(
        lambda *arrays: tuple(local(*arrays)),
        mesh=mesh,
        in_specs=(
            P(None, "band", "trial"),
            P("band", None, None),
            P(),
            P("trial", None),
            P("trial", None),
            P(),
        ),
        out_specs=(P(None, ("trial", "band"), None), P(None, ("trial", "band"), None)),
        check_vma=False,
    )
```

```python
import functools
import math

import jax
import jax.numpy as jnp
from jax import lax
from jax.experimental import pallas as pl
from jax.experimental.pallas import tpu as pltpu
from jax.sharding import PartitionSpec as P

QSPAN = 4
MAXD1 = 32
LANES = 128


def round_up(number, step):
    return (number + step - 1) // step * step


def fine_kernel(trial_ranges, span_any, x_hbm, delay_hbm, *refs):
    (keep_ref, swap_ref, x_ref, delay_ref, turned_ref, lagged_ref, joined_ref, tail_ref, span_ref, sems) = refs
    subs, beams, width, block_len = x_ref.shape
    q_count = delay_ref.shape[1]
    packed = LANES // q_count
    step = MAXD1 // 2
    tiles = step // packed
    halves = block_len // LANES
    reach = MAXD1 + block_len
    unit = trial_ranges * QSPAN * packed
    per_range = QSPAN * packed
    lead = min(3, subs)
    early = 1
    copies = [
        pltpu.make_async_copy(x_hbm.at[:, pl.ds(sub * width, width), :], x_ref.at[sub], sems.at[sub])
        for sub in range(subs)
    ]
    delay_copies = [
        pltpu.make_async_copy(delay_hbm.at[pl.ds(0, early)], delay_ref.at[pl.ds(0, early)], sems.at[subs]),
        pltpu.make_async_copy(delay_hbm.at[pl.ds(early, subs - early)], delay_ref.at[pl.ds(early, subs - early)], sems.at[subs + 1]),
    ]
    span_copy = pltpu.make_async_copy(span_any, span_ref, sems.at[subs + 2])
    delay_copies[0].start()
    copies[0].start()
    span_copy.start()
    copies[1].start()
    delay_copies[1].start()
    for sub in range(2, lead):
        copies[sub].start()
    for parity in range(turned_ref.shape[0]):
        for beam in range(beams):
            turned_ref[parity, beam, :step, :] = jnp.zeros((step, width), jnp.bfloat16)
            turned_ref[parity, beam, step + block_len :, :] = jnp.zeros((step, width), jnp.bfloat16)
    for parity in range(lagged_ref.shape[0]):
        for beam in range(beams):
            lagged_ref[parity, beam, :step, :] = jnp.zeros((step, step * q_count), jnp.float32)
            lagged_ref[parity, beam, reach:, :] = jnp.zeros((step, step * q_count), jnp.float32)
    joined_ref[:, :, reach:, :] = jnp.zeros((subs, beams, 8, LANES), jnp.float32)
    lane_part = (lax.broadcasted_iota(jnp.int32, (width, LANES), 1) // q_count).astype(jnp.float32)
    own = lax.axis_index("band") * subs
    me = lax.axis_index("trial")
    lane = lax.broadcasted_iota(jnp.int32, (8, LANES), 1)
    row_id = lax.broadcasted_iota(jnp.int32, (QSPAN * packed, LANES), 0)
    lane_id = lax.broadcasted_iota(jnp.int32, (QSPAN * packed, LANES), 1)
    tail_row = lax.broadcasted_iota(jnp.int32, (trial_ranges * packed, LANES), 0)
    tail_lane = lax.broadcasted_iota(jnp.int32, (trial_ranges * packed, LANES), 1)
    def one_sub(sub):
        if sub == 0:
            delay_copies[0].wait()
        if sub == early:
            delay_copies[1].wait()
        tiled = jnp.concatenate([delay_ref[sub]] * packed, axis=0).astype(jnp.float32).T - lane_part
        selector = jnp.concatenate(
            [
                jnp.concatenate(
                    [
                        jnp.where(tiled == jnp.float32(half * step + tile * packed), 1.0, 0.0).astype(jnp.bfloat16)
                        for tile in range(tiles)
                    ],
                    axis=1,
                )
                for half in range(2)
            ],
            axis=0,
        )
        copies[sub].wait()
        if sub + lead < subs:
            copies[sub + lead].start()
        side, other = sub % turned_ref.shape[0], sub % lagged_ref.shape[0]
        left = []
        for beam in range(beams):
            turned_ref[side, beam, step : step + block_len, :] = x_ref[sub, beam].T
            left.append(
                jnp.concatenate(
                    [turned_ref[side, beam, : step + block_len, :], turned_ref[side, beam, step : 2 * step + block_len, :]],
                    axis=1,
                )
            )
        both = jnp.dot(jnp.concatenate(left, axis=0), selector, preferred_element_type=jnp.float32)
        for beam in range(beams):
            lagged_ref[other, beam, step:reach, :] = both[beam * (step + block_len) : (beam + 1) * (step + block_len)]
        for beam in range(beams):
            for start in range(0, reach, 8):
                total = lagged_ref[other, beam, start : start + 8, :LANES]
                for tile in range(1, tiles):
                    at = start + packed * tile
                    total = total + lagged_ref[other, beam, at : at + 8, tile * LANES : (tile + 1) * LANES]
                joined_ref[sub, beam, start : start + 8, :] = total

    def choose(group):
        if group == 0:
            span_copy.wait()
        firsts = [[span_ref[me ^ target, own + group * packed + place] for place in range(packed)] for target in range(trial_ranges)]
        chooser = []
        for target in range(trial_ranges):
            column = jnp.zeros((per_range, LANES), jnp.int32)
            for place in range(packed):
                column = jnp.where(row_id % packed == place, firsts[target][place] + place * q_count, column)
            chooser.append((lane_id == column + row_id // packed).astype(jnp.float32))
        chooser = jnp.concatenate(chooser, axis=0).astype(jnp.bfloat16)
        tail_column = jnp.zeros((trial_ranges * packed, LANES), jnp.int32)
        for target in range(trial_ranges):
            for place in range(packed):
                tail_column = jnp.where(tail_row == target * packed + place, firsts[target][place] + place * q_count, tail_column)
        tail_chooser = jnp.concatenate([(tail_lane == tail_column + span).astype(jnp.float32) for span in range(QSPAN)], axis=0).astype(jnp.bfloat16)
        for beam in range(beams):
            pieces = []
            for start in list(range(MAXD1, reach, 8)) + list(range(0, MAXD1, 8)):
                total = None
                for turn in range(packed):
                    mixed = None
                    for part in range(packed):
                        there = (part + turn) % packed
                        piece = joined_ref[group * packed + there, beam, start + part : start + part + 8, :]
                        mixed = piece if mixed is None else jnp.where(lane >= part * q_count, piece, mixed)
                    if turn:
                        mixed = pltpu.roll(mixed, turn * q_count, 1)
                    total = mixed if total is None else total + mixed
                pieces.append(total)
            rows = jnp.concatenate(pieces, axis=0).astype(jnp.bfloat16)
            chosen = lax.dot_general(
                chooser, rows[:block_len], (((1,), (1,)), ((), ())), preferred_element_type=jnp.float32
            ).astype(jnp.bfloat16)
            for target in range(trial_ranges):
                for half in range(halves):
                    at = ((group * beams + beam) * halves + half) * per_range
                    (keep_ref, swap_ref)[target % 2][target // 2, at : at + per_range, :] = chosen[
                        target * per_range : (target + 1) * per_range, half * LANES : (half + 1) * LANES
                    ]
            tails = lax.dot_general(
                tail_chooser, rows[block_len:], (((1,), (1,)), ((), ())), preferred_element_type=jnp.float32
            )
            units = trial_ranges * packed
            tails = jnp.concatenate([tails[span * units : (span + 1) * units] for span in range(QSPAN)], axis=1)
            for target in range(trial_ranges):
                tail_ref[target, pl.ds((group * beams + beam) * packed, packed), :] = tails[target * packed : (target + 1) * packed]

    for sub in range(subs):
        one_sub(sub)
        if sub and sub % packed == 0:
            choose(sub // packed - 1)
    choose(subs // packed - 1)
    main = subs * beams * halves * QSPAN
    for target in range(trial_ranges):
        (keep_ref, swap_ref)[target % 2][target // 2, main:, :] = tail_ref[target].astype(jnp.bfloat16)


def pair_kernel(keep_ref, swap_ref, *out_refs):
    for place, out_ref in enumerate(out_refs):
        out_ref[0] = keep_ref[place]
        out_ref[1] = swap_ref[place]


def spread(subs, beams, packed, recv_refs, wide_ref, flat_ref):
    _, rows, _ = recv_refs[0].shape
    sources = 2 * len(recv_refs)
    halves = 2
    blocks = sources * halves
    main = subs * beams * halves * QSPAN
    me = lax.axis_index("trial")
    for step in range(sources):
        at = pl.multiple_of((me ^ step) * rows, 16)
        flat_ref[pl.ds(at, rows), :] = recv_refs[-1 - step // 2][step % 2].astype(jnp.float32)
    flat_ref[sources * rows :] = jnp.zeros((rows, LANES), jnp.float32)
    lane = lax.broadcasted_iota(jnp.int32, (sources, LANES), 1)
    for pair in range(subs * beams):
        sub, beam = pair // beams, pair % beams
        group, inside = sub // packed, sub % packed
        tail_at = main + (group * beams + beam) * packed + inside
        tails = flat_ref[pl.ds(rows + tail_at, sources, stride=rows), :]
        for span in range(QSPAN):
            row = pair * QSPAN + span
            wide_ref[row, blocks:, :] = jnp.zeros((wide_ref.shape[1] - blocks, LANES), jnp.float32)
            for half in range(halves):
                place = (((group * beams + beam) * halves + half) * QSPAN + span) * packed + inside
                piece = flat_ref[pl.ds(place, sources, stride=rows), :]
                if half == halves - 1:
                    turn = (LANES - MAXD1 - span * MAXD1) % LANES
                    moved = pltpu.roll(tails, turn, 1) if turn else tails
                    piece = piece + jnp.where(lane >= LANES - MAXD1, moved, 0.0)
                wide_ref[row, pl.ds(half, sources, stride=halves), :] = piece


def add_trials(subs, beams, first, count, place_ref, wide_ref, sums_ref, out_ref):
    blocks = sums_ref.shape[0] // (beams * count)
    lane = lax.broadcasted_iota(jnp.int32, (8, LANES), 1)

    def one_trial(inside, carry):
        sums = [[None] * (blocks // 8) for _ in range(beams)]
        for sub in range(subs):
            place = place_ref[sub, first + inside]
            row = place >> 20
            coarse = (place >> 7) & 0x1FFF
            fine = place & (LANES - 1)
            keep = lane >= fine
            turn = (LANES - fine) & (LANES - 1)
            for beam in range(beams):
                for part in range(blocks // 8):
                    at = coarse + part * 8
                    near = wide_ref[row + beam * QSPAN, pl.ds(at, 8), :]
                    far = wide_ref[row + beam * QSPAN, pl.ds(at + 1, 8), :]
                    moved = pltpu.roll(jnp.where(keep, near, far), turn, 1)
                    held = sums[beam][part]
                    sums[beam][part] = moved if held is None else held + moved
        for beam in range(beams):
            for part in range(blocks // 8):
                start = part * 8 * beams * count + beam * count + inside
                sums_ref[pl.ds(start, 8, stride=beams * count), :] = sums[beam][part]
        return carry

    lax.fori_loop(0, count, one_trial, 0, unroll=min(count, 8))
    out_ref[...] = sums_ref[...].reshape(out_ref.shape).astype(out_ref.dtype)


def partner(place, step, peers):
    return place ^ step if peers & (peers - 1) == 0 else (place + step) % peers


def first_kernel(subs, beams, packed, bands, step, count, place_any, *refs):
    wide_ref, out_ref, flat_ref, sums_ref, place_ref, sem = refs[-6:]
    place_copy = pltpu.make_async_copy(place_any, place_ref, sem)
    place_copy.start()
    spread(subs, beams, packed, refs[:-6], wide_ref, flat_ref)
    place_copy.wait()
    band = partner(lax.axis_index("band"), step, bands)
    add_trials(subs, beams, band * count, count, place_ref, wide_ref, sums_ref, out_ref)


def next_kernel(subs, beams, bands, steps, count, place_ref, wide_ref, *refs):
    for step, out_ref in zip(steps, refs):
        band = partner(lax.axis_index("band"), step, bands)
        add_trials(subs, beams, band * count, count, place_ref, wide_ref, refs[-1], out_ref)


def peak_kernel(beams, scale, width_any, *refs):
    x_refs, (series_ref, peak_ref, width_ref, sem) = refs[:-4], refs[-4:]
    width_copy = pltpu.make_async_copy(width_any, width_ref, sem)
    width_copy.start()
    blocks, rows, _ = x_refs[0].shape
    per_beam = rows // beams
    series = []
    for block in range(blocks):
        total = x_refs[0][block].astype(jnp.float32)
        for x_ref in x_refs[1:]:
            total = total + x_ref[block].astype(jnp.float32)
        series.append((total / scale).astype(jnp.bfloat16))
    for block in range(blocks):
        for beam in range(beams):
            series_ref[beam, :, block * LANES : (block + 1) * LANES] = (
                series[block].astype(jnp.float32)[beam * per_beam : (beam + 1) * per_beam].astype(jnp.bfloat16)
            )
    following = series[1:] + [jnp.zeros_like(series[0])]
    left = jnp.concatenate(
        [jnp.concatenate([here, after], axis=1) for here, after in zip(series, following)], axis=0
    )
    width_copy.wait()
    source = lax.broadcasted_iota(jnp.int32, (2 * LANES, LANES), 0)
    place = lax.broadcasted_iota(jnp.int32, (2 * LANES, LANES), 1)
    for slot in range(peak_ref.shape[1]):
        width = width_ref[slot]
        window = ((source >= place) & (source < place + width)).astype(jnp.bfloat16)
        totals = jnp.dot(left, window, preferred_element_type=jnp.float32)
        best = totals[:rows]
        for block in range(1, blocks):
            best = jnp.maximum(best, totals[block * rows : (block + 1) * rows])
        root = jnp.sqrt(jnp.full((1, rows), width, jnp.int32).astype(jnp.float32))
        peaks = jnp.max(best.T, axis=0, keepdims=True) / root
        for beam in range(beams):
            peak_ref[beam, slot : slot + 1, :] = peaks[:, beam * per_beam : (beam + 1) * per_beam]


def local(intensity, fine_delay, span_start, sub_rel, offset, widths):
    beams, channels, block_len = intensity.shape
    subs, q_count, width = fine_delay.shape
    sources = lax.axis_size("trial")
    bands = lax.axis_size("band")
    trials = sub_rel.shape[0]
    halves = block_len // LANES
    packed = LANES // q_count
    blocks = sources * halves
    length = sources * block_len
    main = subs * beams * halves * QSPAN
    rows = round_up(main + subs * beams, 16)
    in_smem = pl.BlockSpec(memory_space=pltpu.SMEM)
    in_vmem = pl.BlockSpec(memory_space=pltpu.VMEM)
    small = pltpu.CompilerParams(vmem_limit_bytes=16 << 20)
    chips = sources // 2
    keep, swap = pl.pallas_call(
        functools.partial(fine_kernel, sources),
        in_specs=[pl.BlockSpec(memory_space=pl.ANY)] * 3,
        out_specs=[in_vmem] * 2,
        scratch_shapes=[
            pltpu.VMEM((subs, beams, width, block_len), jnp.bfloat16),
            pltpu.VMEM((subs, q_count, width), jnp.int32),
            pltpu.VMEM((1, beams, block_len + MAXD1, width), jnp.bfloat16),
            pltpu.VMEM((1, beams, block_len + MAXD1 + MAXD1 // 2, MAXD1 // 2 * q_count), jnp.float32),
            pltpu.VMEM((subs, beams, block_len + MAXD1 + 8, LANES), jnp.float32),
            pltpu.VMEM((sources, rows - main, LANES), jnp.float32),
            pltpu.SMEM(span_start.shape, jnp.int32),
            pltpu.SemaphoreType.DMA((subs + 3,)),
        ],
        out_shape=[pltpu.VMEM((chips, rows, LANES), jnp.bfloat16)] * 2,
        compiler_params=pltpu.CompilerParams(vmem_limit_bytes=61 << 20),
        name="fine_delays",
    )(span_start, intensity, fine_delay)
    own = lax.axis_index("band") * subs
    own_rel = lax.dynamic_slice_in_dim(sub_rel.T, own, subs, 0)
    own_shift = lax.dynamic_slice_in_dim(offset.T, own, subs, 0)
    pair = jnp.arange(subs, dtype=jnp.int32)[:, None] * beams
    places = ((pair * QSPAN + own_rel) << 20) + own_shift

    def crossed(array, step):
        return lax.ppermute(array, "trial", [(place, place ^ step) for place in range(sources)])

    pairs = pl.pallas_call(
        pair_kernel,
        in_specs=[in_vmem] * 2,
        out_specs=[in_vmem] * chips,
        out_shape=[jax.ShapeDtypeStruct((2, rows, LANES), jnp.bfloat16)] * chips,
        compiler_params=small,
        name="pair_rows",
    )(keep, crossed(swap, 1))
    received = [crossed(pairs[step], 2 * step) for step in range(chips - 1, 0, -1)] + [pairs[0]]
    stride = round_up(blocks + length // 2 // LANES + 1, 8)
    count = trials // bands
    chunk_shape = (blocks, beams * count, LANES)
    sums_scratch = pltpu.VMEM((blocks * beams * count, LANES), jnp.float32)
    steps = list(range(bands - 1, -1, -1))
    wide, first = pl.pallas_call(
        functools.partial(first_kernel, subs, beams, packed, bands, steps[0], count),
        in_specs=[pl.BlockSpec(memory_space=pl.ANY)] + [in_vmem] * chips,
        out_specs=[in_vmem, in_vmem],
        scratch_shapes=[
            pltpu.VMEM(((sources + 1) * rows, LANES), jnp.float32),
            sums_scratch,
            pltpu.SMEM(places.shape, jnp.int32),
            pltpu.SemaphoreType.DMA,
        ],
        out_shape=[jax.ShapeDtypeStruct((subs * beams * QSPAN, stride, LANES), jnp.float32), jax.ShapeDtypeStruct(chunk_shape, jnp.bfloat16)],
        compiler_params=small,
        name="spread_and_add",
    )(places, *received)
    later = steps[1:]
    kinds = [jnp.bfloat16 if step % 2 else jnp.float32 for step in later]
    rest = pl.pallas_call(
        functools.partial(next_kernel, subs, beams, bands, later, count),
        in_specs=[in_smem, in_vmem],
        out_specs=[in_vmem] * len(later),
        scratch_shapes=[sums_scratch],
        out_shape=[jax.ShapeDtypeStruct(chunk_shape, kind) for kind in kinds],
        compiler_params=small,
        cost_estimate=pl.CostEstimate(flops=4 << 30, bytes_accessed=12 << 20, transcendentals=0),
        name="add_trials",
    )(places, wide)

    def sent(sums, step):
        return lax.ppermute(sums, "band", [(place, partner(place, step, bands)) for place in range(bands)])

    chunks = dict(zip(steps, [first] + list(rest)))
    arrived = [chunks[0]]
    for step in range(2, bands, 2):
        from_pair = sent(chunks[step + 1], 1).astype(jnp.float32)
        arrived.append(sent((chunks[step] + from_pair).astype(jnp.bfloat16), step))
    arrived.append(sent(chunks[1], 1))
    series, peaks = pl.pallas_call(
        functools.partial(peak_kernel, beams, math.sqrt(channels * bands)),
        in_specs=[pl.BlockSpec(memory_space=pl.ANY)] + [in_vmem] * len(arrived),
        out_specs=[in_vmem] * 2,
        scratch_shapes=[pltpu.SMEM(widths.shape, jnp.int32), pltpu.SemaphoreType.DMA],
        out_shape=[
            jax.ShapeDtypeStruct((beams, count, length), jnp.bfloat16),
            jax.ShapeDtypeStruct((beams, widths.shape[0], count), jnp.float32),
        ],
        compiler_params=small,
        name="boxcar_peaks",
    )(widths, *arrived)
    return series, peaks.swapaxes(1, 2)


def solution(mesh):
    return jax.shard_map(
        lambda *arrays: tuple(local(*arrays)),
        mesh=mesh,
        in_specs=(
            P(None, "band", "trial"),
            P("band", None, None),
            P(),
            P("trial", None),
            P("trial", None),
            P(),
        ),
        out_specs=(P(None, ("trial", "band"), None), P(None, ("trial", "band"), None)),
        check_vma=False,
    )
```

```python
import functools
import math

import jax
import jax.numpy as jnp
from jax import lax
from jax.experimental import pallas as pl
from jax.experimental.pallas import tpu as pltpu
from jax.sharding import PartitionSpec as P

QSPAN = 4
MAXD1 = 32
LANES = 128


def round_up(number, step):
    return (number + step - 1) // step * step


def fine_kernel(trial_ranges, span_any, x_hbm, delay_hbm, *refs):
    (keep_ref, swap_ref, x_ref, delay_ref, turned_ref, lagged_ref, joined_ref, tail_ref, span_ref, sems) = refs
    subs, beams, width, block_len = x_ref.shape
    q_count = delay_ref.shape[1]
    packed = LANES // q_count
    step = MAXD1 // 2
    tiles = step // packed
    halves = block_len // LANES
    reach = MAXD1 + block_len
    unit = trial_ranges * QSPAN * packed
    per_range = QSPAN * packed
    lead = min(3, subs)
    early = 1
    copies = [
        pltpu.make_async_copy(x_hbm.at[:, pl.ds(sub * width, width), :], x_ref.at[sub], sems.at[sub])
        for sub in range(subs)
    ]
    delay_copies = [
        pltpu.make_async_copy(delay_hbm.at[pl.ds(0, early)], delay_ref.at[pl.ds(0, early)], sems.at[subs]),
        pltpu.make_async_copy(delay_hbm.at[pl.ds(early, subs - early)], delay_ref.at[pl.ds(early, subs - early)], sems.at[subs + 1]),
    ]
    span_copy = pltpu.make_async_copy(span_any, span_ref, sems.at[subs + 2])
    delay_copies[0].start()
    copies[0].start()
    span_copy.start()
    copies[1].start()
    delay_copies[1].start()
    for sub in range(2, lead):
        copies[sub].start()
    for parity in range(turned_ref.shape[0]):
        for beam in range(beams):
            turned_ref[parity, beam, :step, :] = jnp.zeros((step, width), jnp.bfloat16)
            turned_ref[parity, beam, step + block_len :, :] = jnp.zeros((step, width), jnp.bfloat16)
    for parity in range(lagged_ref.shape[0]):
        for beam in range(beams):
            lagged_ref[parity, beam, :step, :] = jnp.zeros((step, step * q_count), jnp.float32)
            lagged_ref[parity, beam, reach:, :] = jnp.zeros((step, step * q_count), jnp.float32)
    joined_ref[:, :, reach:, :] = jnp.zeros((subs, beams, 8, LANES), jnp.float32)
    lane_part = (lax.broadcasted_iota(jnp.int32, (width, LANES), 1) // q_count).astype(jnp.float32)
    own = lax.axis_index("band") * subs
    me = lax.axis_index("trial")
    lane = lax.broadcasted_iota(jnp.int32, (8, LANES), 1)
    row_id = lax.broadcasted_iota(jnp.int32, (QSPAN * packed, LANES), 0)
    lane_id = lax.broadcasted_iota(jnp.int32, (QSPAN * packed, LANES), 1)
    tail_row = lax.broadcasted_iota(jnp.int32, (trial_ranges * packed, LANES), 0)
    tail_lane = lax.broadcasted_iota(jnp.int32, (trial_ranges * packed, LANES), 1)
    def one_sub(sub):
        if sub == 0:
            delay_copies[0].wait()
        if sub == early:
            delay_copies[1].wait()
        tiled = jnp.concatenate([delay_ref[sub]] * packed, axis=0).astype(jnp.float32).T - lane_part
        selector = jnp.concatenate(
            [
                jnp.concatenate(
                    [
                        jnp.where(tiled == jnp.float32(half * step + tile * packed), 1.0, 0.0).astype(jnp.bfloat16)
                        for tile in range(tiles)
                    ],
                    axis=1,
                )
                for half in range(2)
            ],
            axis=0,
        )
        copies[sub].wait()
        if sub + lead < subs:
            copies[sub + lead].start()
        side, other = sub % turned_ref.shape[0], sub % lagged_ref.shape[0]
        left = []
        for beam in range(beams):
            turned_ref[side, beam, step : step + block_len, :] = x_ref[sub, beam].T
            left.append(
                jnp.concatenate(
                    [turned_ref[side, beam, : step + block_len, :], turned_ref[side, beam, step : 2 * step + block_len, :]],
                    axis=1,
                )
            )
        both = jnp.dot(jnp.concatenate(left, axis=0), selector, preferred_element_type=jnp.float32)
        for beam in range(beams):
            lagged_ref[other, beam, step:reach, :] = both[beam * (step + block_len) : (beam + 1) * (step + block_len)]
        for beam in range(beams):
            for start in range(0, reach, 8):
                total = lagged_ref[other, beam, start : start + 8, :LANES]
                for tile in range(1, tiles):
                    at = start + packed * tile
                    total = total + lagged_ref[other, beam, at : at + 8, tile * LANES : (tile + 1) * LANES]
                joined_ref[sub, beam, start : start + 8, :] = total

    def choose(group):
        if group == 0:
            span_copy.wait()
        firsts = [[span_ref[me ^ target, own + group * packed + place] for place in range(packed)] for target in range(trial_ranges)]
        chooser = []
        for target in range(trial_ranges):
            column = jnp.zeros((per_range, LANES), jnp.int32)
            for place in range(packed):
                column = jnp.where(row_id % packed == place, firsts[target][place] + place * q_count, column)
            chooser.append((lane_id == column + row_id // packed).astype(jnp.float32))
        chooser = jnp.concatenate(chooser, axis=0).astype(jnp.bfloat16)
        tail_column = jnp.zeros((trial_ranges * packed, LANES), jnp.int32)
        for target in range(trial_ranges):
            for place in range(packed):
                tail_column = jnp.where(tail_row == target * packed + place, firsts[target][place] + place * q_count, tail_column)
        tail_chooser = jnp.concatenate([(tail_lane == tail_column + span).astype(jnp.float32) for span in range(QSPAN)], axis=0).astype(jnp.bfloat16)
        for beam in range(beams):
            pieces = []
            for start in list(range(MAXD1, reach, 8)) + list(range(0, MAXD1, 8)):
                total = None
                for turn in range(packed):
                    mixed = None
                    for part in range(packed):
                        there = (part + turn) % packed
                        piece = joined_ref[group * packed + there, beam, start + part : start + part + 8, :]
                        mixed = piece if mixed is None else jnp.where(lane >= part * q_count, piece, mixed)
                    if turn:
                        mixed = pltpu.roll(mixed, turn * q_count, 1)
                    total = mixed if total is None else total + mixed
                pieces.append(total)
            rows = jnp.concatenate(pieces, axis=0).astype(jnp.bfloat16)
            chosen = lax.dot_general(
                chooser, rows[:block_len], (((1,), (1,)), ((), ())), preferred_element_type=jnp.float32
            ).astype(jnp.bfloat16)
            for target in range(trial_ranges):
                for half in range(halves):
                    at = ((group * beams + beam) * halves + half) * per_range
                    (keep_ref, swap_ref)[target % 2][target // 2, at : at + per_range, :] = chosen[
                        target * per_range : (target + 1) * per_range, half * LANES : (half + 1) * LANES
                    ]
            tails = lax.dot_general(
                tail_chooser, rows[block_len:], (((1,), (1,)), ((), ())), preferred_element_type=jnp.float32
            )
            units = trial_ranges * packed
            tails = jnp.concatenate([tails[span * units : (span + 1) * units] for span in range(QSPAN)], axis=1)
            for target in range(trial_ranges):
                tail_ref[target, pl.ds((group * beams + beam) * packed, packed), :] = tails[target * packed : (target + 1) * packed]

    for sub in range(subs):
        one_sub(sub)
        if sub and sub % packed == 0:
            choose(sub // packed - 1)
    choose(subs // packed - 1)
    main = subs * beams * halves * QSPAN
    for target in range(trial_ranges):
        (keep_ref, swap_ref)[target % 2][target // 2, main:, :] = tail_ref[target].astype(jnp.bfloat16)


def pair_kernel(keep_ref, swap_ref, *out_refs):
    for place, out_ref in enumerate(out_refs):
        out_ref[0] = keep_ref[place]
        out_ref[1] = swap_ref[place]


def spread(subs, beams, packed, recv_refs, wide_ref, flat_ref):
    _, rows, _ = recv_refs[0].shape
    sources = 2 * len(recv_refs)
    halves = 2
    blocks = sources * halves
    main = subs * beams * halves * QSPAN
    me = lax.axis_index("trial")
    for step in range(sources):
        at = pl.multiple_of((me ^ step) * rows, 16)
        flat_ref[pl.ds(at, rows), :] = recv_refs[-1 - step // 2][step % 2].astype(jnp.float32)
    flat_ref[sources * rows :] = jnp.zeros((rows, LANES), jnp.float32)
    lane = lax.broadcasted_iota(jnp.int32, (sources, LANES), 1)
    for pair in range(subs * beams):
        sub, beam = pair // beams, pair % beams
        group, inside = sub // packed, sub % packed
        tail_at = main + (group * beams + beam) * packed + inside
        tails = flat_ref[pl.ds(rows + tail_at, sources, stride=rows), :]
        for span in range(QSPAN):
            row = pair * QSPAN + span
            wide_ref[row, blocks:, :] = jnp.zeros((wide_ref.shape[1] - blocks, LANES), jnp.float32)
            for half in range(halves):
                place = (((group * beams + beam) * halves + half) * QSPAN + span) * packed + inside
                piece = flat_ref[pl.ds(place, sources, stride=rows), :]
                if half == halves - 1:
                    turn = (LANES - MAXD1 - span * MAXD1) % LANES
                    moved = pltpu.roll(tails, turn, 1) if turn else tails
                    piece = piece + jnp.where(lane >= LANES - MAXD1, moved, 0.0)
                wide_ref[row, pl.ds(half, sources, stride=halves), :] = piece


def add_trials(subs, beams, first, count, place_ref, wide_ref, sums_ref, out_ref):
    blocks = sums_ref.shape[0] // (beams * count)
    lane = lax.broadcasted_iota(jnp.int32, (8, LANES), 1)

    def one_trial(inside, carry):
        sums = [[None] * (blocks // 8) for _ in range(beams)]
        for sub in range(subs):
            place = place_ref[sub, first + inside]
            row = place >> 20
            coarse = (place >> 7) & 0x1FFF
            fine = place & (LANES - 1)
            keep = lane >= fine
            turn = (LANES - fine) & (LANES - 1)
            for beam in range(beams):
                for part in range(blocks // 8):
                    at = coarse + part * 8
                    near = wide_ref[row + beam * QSPAN, pl.ds(at, 8), :]
                    far = wide_ref[row + beam * QSPAN, pl.ds(at + 1, 8), :]
                    moved = pltpu.roll(jnp.where(keep, near, far), turn, 1)
                    held = sums[beam][part]
                    sums[beam][part] = moved if held is None else held + moved
        for beam in range(beams):
            for part in range(blocks // 8):
                start = part * 8 * beams * count + beam * count + inside
                sums_ref[pl.ds(start, 8, stride=beams * count), :] = sums[beam][part]
        return carry

    lax.fori_loop(0, count, one_trial, 0, unroll=min(count, 16))
    out_ref[...] = sums_ref[...].reshape(out_ref.shape).astype(out_ref.dtype)


def partner(place, step):
    return place ^ step


def first_kernel(subs, beams, packed, step, count, place_any, *refs):
    wide_ref, out_ref, flat_ref, sums_ref, place_ref, sem = refs[-6:]
    place_copy = pltpu.make_async_copy(place_any, place_ref, sem)
    place_copy.start()
    spread(subs, beams, packed, refs[:-6], wide_ref, flat_ref)
    place_copy.wait()
    band = partner(lax.axis_index("band"), step)
    add_trials(subs, beams, band * count, count, place_ref, wide_ref, sums_ref, out_ref)


def next_kernel(subs, beams, steps, count, place_ref, wide_ref, *refs):
    for step, out_ref in zip(steps, refs):
        band = partner(lax.axis_index("band"), step)
        add_trials(subs, beams, band * count, count, place_ref, wide_ref, refs[-1], out_ref)


def peak_kernel(beams, scale, width_any, *refs):
    x_refs, (series_ref, peak_ref, width_ref, sem) = refs[:-4], refs[-4:]
    width_copy = pltpu.make_async_copy(width_any, width_ref, sem)
    width_copy.start()
    blocks, rows, _ = x_refs[0].shape
    per_beam = rows // beams
    series = []
    for block in range(blocks):
        total = x_refs[0][block].astype(jnp.float32)
        for x_ref in x_refs[1:]:
            total = total + x_ref[block].astype(jnp.float32)
        series.append((total / scale).astype(jnp.bfloat16))
    for block in range(blocks):
        for beam in range(beams):
            series_ref[beam, :, block * LANES : (block + 1) * LANES] = (
                series[block].astype(jnp.float32)[beam * per_beam : (beam + 1) * per_beam].astype(jnp.bfloat16)
            )
    following = series[1:] + [jnp.zeros_like(series[0])]
    left = jnp.concatenate(
        [jnp.concatenate([here, after], axis=1) for here, after in zip(series, following)], axis=0
    )
    width_copy.wait()
    source = lax.broadcasted_iota(jnp.int32, (2 * LANES, LANES), 0)
    place = lax.broadcasted_iota(jnp.int32, (2 * LANES, LANES), 1)
    slots = peak_ref.shape[1]
    window = jnp.concatenate(
        [
            jnp.where((source >= place) & (source < place + width_ref[slot]), 1.0, 0.0).astype(jnp.bfloat16)
            for slot in range(slots)
        ],
        axis=1,
    )
    best = None
    for block in range(0, blocks, 4):
        totals = jnp.dot(left[block * rows : (block + 4) * rows], window, preferred_element_type=jnp.float32)
        for inside in range(4):
            piece = totals[inside * rows : (inside + 1) * rows]
            best = piece if best is None else jnp.maximum(best, piece)
    for slot in range(slots):
        root = jnp.sqrt(jnp.full((1, rows), width_ref[slot], jnp.int32).astype(jnp.float32))
        peaks = jnp.max(best[:, slot * LANES : (slot + 1) * LANES].T, axis=0, keepdims=True) / root
        for beam in range(beams):
            peak_ref[beam, slot : slot + 1, :] = peaks[:, beam * per_beam : (beam + 1) * per_beam]


def local(intensity, fine_delay, span_start, sub_rel, offset, widths):
    beams, channels, block_len = intensity.shape
    subs, q_count, width = fine_delay.shape
    sources = lax.axis_size("trial")
    bands = lax.axis_size("band")
    trials = sub_rel.shape[0]
    halves = block_len // LANES
    packed = LANES // q_count
    blocks = sources * halves
    length = sources * block_len
    main = subs * beams * halves * QSPAN
    rows = round_up(main + subs * beams, 16)
    in_smem = pl.BlockSpec(memory_space=pltpu.SMEM)
    in_vmem = pl.BlockSpec(memory_space=pltpu.VMEM)
    small = pltpu.CompilerParams(vmem_limit_bytes=16 << 20)
    chips = sources // 2
    keep, swap = pl.pallas_call(
        functools.partial(fine_kernel, sources),
        in_specs=[pl.BlockSpec(memory_space=pl.ANY)] * 3,
        out_specs=[in_vmem] * 2,
        scratch_shapes=[
            pltpu.VMEM((subs, beams, width, block_len), jnp.bfloat16),
            pltpu.VMEM((subs, q_count, width), jnp.int32),
            pltpu.VMEM((1, beams, block_len + MAXD1, width), jnp.bfloat16),
            pltpu.VMEM((1, beams, block_len + MAXD1 + MAXD1 // 2, MAXD1 // 2 * q_count), jnp.float32),
            pltpu.VMEM((subs, beams, block_len + MAXD1 + 8, LANES), jnp.float32),
            pltpu.VMEM((sources, rows - main, LANES), jnp.float32),
            pltpu.SMEM(span_start.shape, jnp.int32),
            pltpu.SemaphoreType.DMA((subs + 3,)),
        ],
        out_shape=[pltpu.VMEM((chips, rows, LANES), jnp.bfloat16)] * 2,
        compiler_params=pltpu.CompilerParams(vmem_limit_bytes=61 << 20),
        name="fine_delays",
    )(span_start, intensity, fine_delay)
    own = lax.axis_index("band") * subs
    own_rel = lax.dynamic_slice_in_dim(sub_rel.T, own, subs, 0)
    own_shift = lax.dynamic_slice_in_dim(offset.T, own, subs, 0)
    pair = jnp.arange(subs, dtype=jnp.int32)[:, None] * beams
    places = ((pair * QSPAN + own_rel) << 20) + own_shift

    def crossed(array, step):
        return lax.ppermute(array, "trial", [(place, place ^ step) for place in range(sources)])

    pairs = pl.pallas_call(
        pair_kernel,
        in_specs=[in_vmem] * 2,
        out_specs=[in_vmem] * chips,
        out_shape=[jax.ShapeDtypeStruct((2, rows, LANES), jnp.bfloat16)] * chips,
        compiler_params=small,
        name="pair_rows",
    )(keep, crossed(swap, 1))
    received = [crossed(pairs[step], 2 * step) for step in range(chips - 1, 0, -1)] + [pairs[0]]
    stride = round_up(blocks + length // 2 // LANES + 1, 8)
    count = trials // bands
    chunk_shape = (blocks, beams * count, LANES)
    sums_scratch = pltpu.VMEM((blocks * beams * count, LANES), jnp.float32)
    steps = list(range(bands - 1, -1, -1))
    wide, first = pl.pallas_call(
        functools.partial(first_kernel, subs, beams, packed, steps[0], count),
        in_specs=[pl.BlockSpec(memory_space=pl.ANY)] + [in_vmem] * chips,
        out_specs=[in_vmem, in_vmem],
        scratch_shapes=[
            pltpu.VMEM(((sources + 1) * rows, LANES), jnp.float32),
            sums_scratch,
            pltpu.SMEM(places.shape, jnp.int32),
            pltpu.SemaphoreType.DMA,
        ],
        out_shape=[jax.ShapeDtypeStruct((subs * beams * QSPAN, stride, LANES), jnp.float32), jax.ShapeDtypeStruct(chunk_shape, jnp.bfloat16)],
        compiler_params=small,
        name="spread_and_add",
    )(places, *received)
    def more(some):
        return pl.pallas_call(
            functools.partial(next_kernel, subs, beams, some, count),
            in_specs=[in_smem, in_vmem],
            out_specs=[in_vmem] * len(some),
            scratch_shapes=[sums_scratch],
            out_shape=[jax.ShapeDtypeStruct(chunk_shape, jnp.bfloat16 if step % 2 else jnp.float32) for step in some],
            compiler_params=small,
            cost_estimate=pl.CostEstimate(flops=len(some) << 30, bytes_accessed=len(some) << 22, transcendentals=0),
            name="add_trials",
        )(places, wide)

    def sent(sums, step):
        return lax.ppermute(sums, "band", [(place, partner(place, step)) for place in range(bands)])

    chunks = dict(zip(steps, [first] + list(more(steps[1:-1]))))
    arrived = list(more([0]))
    for step in range(2, bands, 2):
        from_pair = sent(chunks[step + 1], 1).astype(jnp.float32)
        arrived.append(sent((chunks[step] + from_pair).astype(jnp.bfloat16), step))
    arrived.append(sent(chunks[1], 1))
    series, peaks = pl.pallas_call(
        functools.partial(peak_kernel, beams, math.sqrt(channels * bands)),
        in_specs=[pl.BlockSpec(memory_space=pl.ANY)] + [in_vmem] * len(arrived),
        out_specs=[in_vmem] * 2,
        scratch_shapes=[pltpu.SMEM(widths.shape, jnp.int32), pltpu.SemaphoreType.DMA],
        out_shape=[
            jax.ShapeDtypeStruct((beams, count, length), jnp.bfloat16),
            jax.ShapeDtypeStruct((beams, widths.shape[0], count), jnp.float32),
        ],
        compiler_params=small,
        name="boxcar_peaks",
    )(widths, *arrived)
    return series, peaks.swapaxes(1, 2)


def solution(mesh):
    return jax.shard_map(
        lambda *arrays: tuple(local(*arrays)),
        mesh=mesh,
        in_specs=(
            P(None, "band", "trial"),
            P("band", None, None),
            P(),
            P("trial", None),
            P("trial", None),
            P(),
        ),
        out_specs=(P(None, ("trial", "band"), None), P(None, ("trial", "band"), None)),
        check_vma=False,
    )
```

```python
import functools
import math

import jax
import jax.numpy as jnp
from jax import lax
from jax.experimental import pallas as pl
from jax.experimental.pallas import tpu as pltpu
from jax.sharding import PartitionSpec as P

QSPAN = 4
MAXD1 = 32
LANES = 128


def round_up(number, step):
    return (number + step - 1) // step * step


def fine_kernel(trial_ranges, span_any, x_hbm, delay_hbm, *refs):
    (keep_ref, swap_ref, x_ref, delay_ref, turned_ref, lagged_ref, joined_ref, tail_ref, span_ref, sems) = refs
    subs, beams, width, block_len = x_ref.shape
    q_count = delay_ref.shape[1]
    packed = LANES // q_count
    step = MAXD1 // 2
    tiles = step // packed
    halves = block_len // LANES
    reach = MAXD1 + block_len
    unit = trial_ranges * QSPAN * packed
    per_range = QSPAN * packed
    lead = min(3, subs)
    early = 1
    copies = [
        pltpu.make_async_copy(x_hbm.at[:, pl.ds(sub * width, width), :], x_ref.at[sub], sems.at[sub])
        for sub in range(subs)
    ]
    delay_copies = [
        pltpu.make_async_copy(delay_hbm.at[pl.ds(0, early)], delay_ref.at[pl.ds(0, early)], sems.at[subs]),
        pltpu.make_async_copy(delay_hbm.at[pl.ds(early, subs - early)], delay_ref.at[pl.ds(early, subs - early)], sems.at[subs + 1]),
    ]
    span_copy = pltpu.make_async_copy(span_any, span_ref, sems.at[subs + 2])
    delay_copies[0].start()
    copies[0].start()
    span_copy.start()
    copies[1].start()
    delay_copies[1].start()
    for sub in range(2, lead):
        copies[sub].start()
    for parity in range(turned_ref.shape[0]):
        for beam in range(beams):
            turned_ref[parity, beam, :step, :] = jnp.zeros((step, width), jnp.bfloat16)
            turned_ref[parity, beam, step + block_len :, :] = jnp.zeros((step, width), jnp.bfloat16)
    for parity in range(lagged_ref.shape[0]):
        for beam in range(beams):
            lagged_ref[parity, beam, :step, :] = jnp.zeros((step, step * q_count), jnp.float32)
            lagged_ref[parity, beam, reach:, :] = jnp.zeros((step, step * q_count), jnp.float32)
    joined_ref[:, :, reach:, :] = jnp.zeros((subs, beams, 8, LANES), jnp.float32)
    lane_part = (lax.broadcasted_iota(jnp.int32, (width, LANES), 1) // q_count).astype(jnp.float32)
    own = lax.axis_index("band") * subs
    me = lax.axis_index("trial")
    lane = lax.broadcasted_iota(jnp.int32, (8, LANES), 1)
    row_id = lax.broadcasted_iota(jnp.int32, (QSPAN * packed, LANES), 0)
    lane_id = lax.broadcasted_iota(jnp.int32, (QSPAN * packed, LANES), 1)
    tail_row = lax.broadcasted_iota(jnp.int32, (trial_ranges * packed, LANES), 0)
    tail_lane = lax.broadcasted_iota(jnp.int32, (trial_ranges * packed, LANES), 1)
    def one_sub(sub):
        if sub == 0:
            delay_copies[0].wait()
        if sub == early:
            delay_copies[1].wait()
        tiled = jnp.concatenate([delay_ref[sub]] * packed, axis=0).astype(jnp.float32).T - lane_part
        selector = jnp.concatenate(
            [
                jnp.concatenate(
                    [
                        jnp.where(tiled == jnp.float32(half * step + tile * packed), 1.0, 0.0).astype(jnp.bfloat16)
                        for tile in range(tiles)
                    ],
                    axis=1,
                )
                for half in range(2)
            ],
            axis=0,
        )
        copies[sub].wait()
        if sub + lead < subs:
            copies[sub + lead].start()
        side, other = sub % turned_ref.shape[0], sub % lagged_ref.shape[0]
        left = []
        for beam in range(beams):
            turned_ref[side, beam, step : step + block_len, :] = x_ref[sub, beam].T
            left.append(
                jnp.concatenate(
                    [turned_ref[side, beam, : step + block_len, :], turned_ref[side, beam, step : 2 * step + block_len, :]],
                    axis=1,
                )
            )
        both = jnp.dot(jnp.concatenate(left, axis=0), selector, preferred_element_type=jnp.float32)
        for beam in range(beams):
            lagged_ref[other, beam, step:reach, :] = both[beam * (step + block_len) : (beam + 1) * (step + block_len)]
        for beam in range(beams):
            for start in range(0, reach, 8):
                total = lagged_ref[other, beam, start : start + 8, :LANES]
                for tile in range(1, tiles):
                    at = start + packed * tile
                    total = total + lagged_ref[other, beam, at : at + 8, tile * LANES : (tile + 1) * LANES]
                joined_ref[sub, beam, start : start + 8, :] = total

    def choose(group):
        if group == 0:
            span_copy.wait()
        firsts = [[span_ref[me ^ target, own + group * packed + place] for place in range(packed)] for target in range(trial_ranges)]
        chooser = []
        for target in range(trial_ranges):
            column = jnp.zeros((per_range, LANES), jnp.int32)
            for place in range(packed):
                column = jnp.where(row_id % packed == place, firsts[target][place] + place * q_count, column)
            chooser.append((lane_id == column + row_id // packed).astype(jnp.float32))
        chooser = jnp.concatenate(chooser, axis=0).astype(jnp.bfloat16)
        tail_column = jnp.zeros((trial_ranges * packed, LANES), jnp.int32)
        for target in range(trial_ranges):
            for place in range(packed):
                tail_column = jnp.where(tail_row == target * packed + place, firsts[target][place] + place * q_count, tail_column)
        tail_chooser = jnp.concatenate([(tail_lane == tail_column + span).astype(jnp.float32) for span in range(QSPAN)], axis=0).astype(jnp.bfloat16)
        for beam in range(beams):
            pieces = []
            for start in list(range(MAXD1, reach, 8)) + list(range(0, MAXD1, 8)):
                total = None
                for turn in range(packed):
                    mixed = None
                    for part in range(packed):
                        there = (part + turn) % packed
                        piece = joined_ref[group * packed + there, beam, start + part : start + part + 8, :]
                        mixed = piece if mixed is None else jnp.where(lane >= part * q_count, piece, mixed)
                    if turn:
                        mixed = pltpu.roll(mixed, turn * q_count, 1)
                    total = mixed if total is None else total + mixed
                pieces.append(total)
            rows = jnp.concatenate(pieces, axis=0).astype(jnp.bfloat16)
            chosen = lax.dot_general(
                chooser, rows[:block_len], (((1,), (1,)), ((), ())), preferred_element_type=jnp.float32
            ).astype(jnp.bfloat16)
            for target in range(trial_ranges):
                for half in range(halves):
                    at = ((group * beams + beam) * halves + half) * per_range
                    (keep_ref, swap_ref)[target % 2][target // 2, at : at + per_range, :] = chosen[
                        target * per_range : (target + 1) * per_range, half * LANES : (half + 1) * LANES
                    ]
            tails = lax.dot_general(
                tail_chooser, rows[block_len:], (((1,), (1,)), ((), ())), preferred_element_type=jnp.float32
            )
            units = trial_ranges * packed
            tails = jnp.concatenate([tails[span * units : (span + 1) * units] for span in range(QSPAN)], axis=1)
            for target in range(trial_ranges):
                tail_ref[target, pl.ds((group * beams + beam) * packed, packed), :] = tails[target * packed : (target + 1) * packed]

    for sub in range(subs):
        one_sub(sub)
        if sub and sub % packed == 0:
            choose(sub // packed - 1)
    choose(subs // packed - 1)
    main = subs * beams * halves * QSPAN
    for target in range(trial_ranges):
        (keep_ref, swap_ref)[target % 2][target // 2, main:, :] = tail_ref[target].astype(jnp.bfloat16)


def pair_kernel(keep_ref, swap_ref, *out_refs):
    for place, out_ref in enumerate(out_refs):
        out_ref[0] = keep_ref[place]
        out_ref[1] = swap_ref[place]


def spread(subs, beams, packed, recv_refs, wide_ref, flat_ref):
    _, rows, _ = recv_refs[0].shape
    sources = 2 * len(recv_refs)
    halves = 2
    blocks = sources * halves
    main = subs * beams * halves * QSPAN
    me = lax.axis_index("trial")
    for step in range(sources):
        at = pl.multiple_of((me ^ step) * rows, 16)
        flat_ref[pl.ds(at, rows), :] = recv_refs[-1 - step // 2][step % 2].astype(jnp.float32)
    flat_ref[sources * rows :] = jnp.zeros((rows, LANES), jnp.float32)
    lane = lax.broadcasted_iota(jnp.int32, (sources, LANES), 1)
    for pair in range(subs * beams):
        sub, beam = pair // beams, pair % beams
        group, inside = sub // packed, sub % packed
        tail_at = main + (group * beams + beam) * packed + inside
        tails = flat_ref[pl.ds(rows + tail_at, sources, stride=rows), :]
        for span in range(QSPAN):
            row = pair * QSPAN + span
            wide_ref[row, blocks:, :] = jnp.zeros((wide_ref.shape[1] - blocks, LANES), jnp.float32)
            for half in range(halves):
                place = (((group * beams + beam) * halves + half) * QSPAN + span) * packed + inside
                piece = flat_ref[pl.ds(place, sources, stride=rows), :]
                if half == halves - 1:
                    turn = (LANES - MAXD1 - span * MAXD1) % LANES
                    moved = pltpu.roll(tails, turn, 1) if turn else tails
                    piece = piece + jnp.where(lane >= LANES - MAXD1, moved, 0.0)
                wide_ref[row, pl.ds(half, sources, stride=halves), :] = piece


def add_trials(subs, beams, first, count, place_ref, wide_ref, sums_ref, out_ref):
    blocks = sums_ref.shape[0] // (beams * count)
    lane = lax.broadcasted_iota(jnp.int32, (8, LANES), 1)

    def one_trial(inside, carry):
        sums = [[None] * (blocks // 8) for _ in range(beams)]
        for sub in range(subs):
            place = place_ref[sub, first + inside]
            row = place >> 20
            coarse = (place >> 7) & 0x1FFF
            fine = place & (LANES - 1)
            keep = lane >= fine
            turn = (LANES - fine) & (LANES - 1)
            for beam in range(beams):
                for part in range(blocks // 8):
                    at = coarse + part * 8
                    near = wide_ref[row + beam * QSPAN, pl.ds(at, 8), :]
                    far = wide_ref[row + beam * QSPAN, pl.ds(at + 1, 8), :]
                    moved = pltpu.roll(jnp.where(keep, near, far), turn, 1)
                    held = sums[beam][part]
                    sums[beam][part] = moved if held is None else held + moved
        for beam in range(beams):
            for part in range(blocks // 8):
                start = part * 8 * beams * count + beam * count + inside
                sums_ref[pl.ds(start, 8, stride=beams * count), :] = sums[beam][part]
        return carry

    lax.fori_loop(0, count, one_trial, 0, unroll=min(count, 16))
    out_ref[...] = sums_ref[...].reshape(out_ref.shape).astype(out_ref.dtype)


def partner(place, step):
    return place ^ step


def first_kernel(subs, beams, packed, step, count, place_any, *refs):
    wide_ref, out_ref, flat_ref, sums_ref, place_ref, sem = refs[-6:]
    place_copy = pltpu.make_async_copy(place_any, place_ref, sem)
    place_copy.start()
    spread(subs, beams, packed, refs[:-6], wide_ref, flat_ref)
    place_copy.wait()
    band = partner(lax.axis_index("band"), step)
    add_trials(subs, beams, band * count, count, place_ref, wide_ref, sums_ref, out_ref)


def next_kernel(subs, beams, steps, count, place_ref, wide_ref, *refs):
    for step, out_ref in zip(steps, refs):
        band = partner(lax.axis_index("band"), step)
        add_trials(subs, beams, band * count, count, place_ref, wide_ref, refs[-1], out_ref)


def peak_kernel(beams, scale, width_any, *refs):
    x_refs, (series_ref, peak_ref, width_ref, sem) = refs[:-4], refs[-4:]
    width_copy = pltpu.make_async_copy(width_any, width_ref, sem)
    width_copy.start()
    blocks, rows, _ = x_refs[0].shape
    per_beam = rows // beams
    series = []
    for block in range(blocks):
        total = x_refs[0][block].astype(jnp.float32)
        for x_ref in x_refs[1:]:
            total = total + x_ref[block].astype(jnp.float32)
        total = total * (1 / scale) if math.frexp(scale)[0] == 0.5 else total / scale
        series.append(total.astype(jnp.bfloat16))
    for block in range(blocks):
        for beam in range(beams):
            series_ref[beam, :, block * LANES : (block + 1) * LANES] = (
                series[block].astype(jnp.float32)[beam * per_beam : (beam + 1) * per_beam].astype(jnp.bfloat16)
            )
    following = series[1:] + [jnp.zeros_like(series[0])]
    left = jnp.concatenate(
        [jnp.concatenate([here, after], axis=1) for here, after in zip(series, following)], axis=0
    )
    width_copy.wait()
    source = lax.broadcasted_iota(jnp.int32, (2 * LANES, LANES), 0)
    place = lax.broadcasted_iota(jnp.int32, (2 * LANES, LANES), 1)
    slots = peak_ref.shape[1]
    window = jnp.concatenate(
        [
            jnp.where((source >= place) & (source < place + width_ref[slot]), 1.0, 0.0).astype(jnp.bfloat16)
            for slot in range(slots)
        ],
        axis=1,
    )
    best = None
    for block in range(0, blocks, 4):
        totals = jnp.dot(left[block * rows : (block + 4) * rows], window, preferred_element_type=jnp.float32)
        for inside in range(4):
            piece = totals[inside * rows : (inside + 1) * rows]
            best = piece if best is None else jnp.maximum(best, piece)
    for slot in range(slots):
        root = jnp.sqrt(jnp.full((1, rows), width_ref[slot], jnp.int32).astype(jnp.float32))
        peaks = jnp.max(best[:, slot * LANES : (slot + 1) * LANES].T, axis=0, keepdims=True) / root
        for beam in range(beams):
            peak_ref[beam, slot : slot + 1, :] = peaks[:, beam * per_beam : (beam + 1) * per_beam]


def local(intensity, fine_delay, span_start, sub_rel, offset, widths):
    beams, channels, block_len = intensity.shape
    subs, q_count, width = fine_delay.shape
    sources = lax.axis_size("trial")
    bands = lax.axis_size("band")
    trials = sub_rel.shape[0]
    halves = block_len // LANES
    packed = LANES // q_count
    blocks = sources * halves
    length = sources * block_len
    main = subs * beams * halves * QSPAN
    rows = round_up(main + subs * beams, 16)
    in_smem = pl.BlockSpec(memory_space=pltpu.SMEM)
    in_vmem = pl.BlockSpec(memory_space=pltpu.VMEM)
    small = pltpu.CompilerParams(vmem_limit_bytes=16 << 20)
    chips = sources // 2
    keep, swap = pl.pallas_call(
        functools.partial(fine_kernel, sources),
        in_specs=[pl.BlockSpec(memory_space=pl.ANY)] * 3,
        out_specs=[in_vmem] * 2,
        scratch_shapes=[
            pltpu.VMEM((subs, beams, width, block_len), jnp.bfloat16),
            pltpu.VMEM((subs, q_count, width), jnp.int32),
            pltpu.VMEM((1, beams, block_len + MAXD1, width), jnp.bfloat16),
            pltpu.VMEM((1, beams, block_len + MAXD1 + MAXD1 // 2, MAXD1 // 2 * q_count), jnp.float32),
            pltpu.VMEM((subs, beams, block_len + MAXD1 + 8, LANES), jnp.float32),
            pltpu.VMEM((sources, rows - main, LANES), jnp.float32),
            pltpu.SMEM(span_start.shape, jnp.int32),
            pltpu.SemaphoreType.DMA((subs + 3,)),
        ],
        out_shape=[pltpu.VMEM((chips, rows, LANES), jnp.bfloat16)] * 2,
        compiler_params=pltpu.CompilerParams(vmem_limit_bytes=61 << 20),
        name="fine_delays",
    )(span_start, intensity, fine_delay)
    own = lax.axis_index("band") * subs
    own_rel = lax.dynamic_slice_in_dim(sub_rel.T, own, subs, 0)
    own_shift = lax.dynamic_slice_in_dim(offset.T, own, subs, 0)
    pair = jnp.arange(subs, dtype=jnp.int32)[:, None] * beams
    places = ((pair * QSPAN + own_rel) << 20) + own_shift

    def crossed(array, step):
        return lax.ppermute(array, "trial", [(place, place ^ step) for place in range(sources)])

    pairs = pl.pallas_call(
        pair_kernel,
        in_specs=[in_vmem] * 2,
        out_specs=[in_vmem] * chips,
        out_shape=[jax.ShapeDtypeStruct((2, rows, LANES), jnp.bfloat16)] * chips,
        compiler_params=small,
        name="pair_rows",
    )(keep, crossed(swap, 1))
    received = [crossed(pairs[step], 2 * step) for step in range(chips - 1, 0, -1)] + [pairs[0]]
    stride = round_up(blocks + length // 2 // LANES + 1, 8)
    count = trials // bands
    chunk_shape = (blocks, beams * count, LANES)
    sums_scratch = pltpu.VMEM((blocks * beams * count, LANES), jnp.float32)
    steps = list(range(bands - 1, -1, -1))
    wide, first = pl.pallas_call(
        functools.partial(first_kernel, subs, beams, packed, steps[0], count),
        in_specs=[pl.BlockSpec(memory_space=pl.ANY)] + [in_vmem] * chips,
        out_specs=[in_vmem, in_vmem],
        scratch_shapes=[
            pltpu.VMEM(((sources + 1) * rows, LANES), jnp.float32),
            sums_scratch,
            pltpu.SMEM(places.shape, jnp.int32),
            pltpu.SemaphoreType.DMA,
        ],
        out_shape=[jax.ShapeDtypeStruct((subs * beams * QSPAN, stride, LANES), jnp.float32), jax.ShapeDtypeStruct(chunk_shape, jnp.bfloat16)],
        compiler_params=small,
        name="spread_and_add",
    )(places, *received)
    def more(some):
        return pl.pallas_call(
            functools.partial(next_kernel, subs, beams, some, count),
            in_specs=[in_smem, in_vmem],
            out_specs=[in_vmem] * len(some),
            scratch_shapes=[sums_scratch],
            out_shape=[jax.ShapeDtypeStruct(chunk_shape, jnp.bfloat16 if step % 2 else jnp.float32) for step in some],
            compiler_params=small,
            cost_estimate=pl.CostEstimate(flops=len(some) << 30, bytes_accessed=len(some) << 22, transcendentals=0),
            name="add_trials",
        )(places, wide)

    def sent(sums, step):
        return lax.ppermute(sums, "band", [(place, partner(place, step)) for place in range(bands)])

    chunks = dict(zip(steps, [first] + list(more(steps[1:-1]))))
    arrived = list(more([0]))
    for step in range(2, bands, 2):
        from_pair = sent(chunks[step + 1], 1).astype(jnp.float32)
        arrived.append(sent((chunks[step] + from_pair).astype(jnp.bfloat16), step))
    arrived.append(sent(chunks[1], 1))
    series, peaks = pl.pallas_call(
        functools.partial(peak_kernel, beams, math.sqrt(channels * bands)),
        in_specs=[pl.BlockSpec(memory_space=pl.ANY)] + [in_vmem] * len(arrived),
        out_specs=[in_vmem] * 2,
        scratch_shapes=[pltpu.SMEM(widths.shape, jnp.int32), pltpu.SemaphoreType.DMA],
        out_shape=[
            jax.ShapeDtypeStruct((beams, count, length), jnp.bfloat16),
            jax.ShapeDtypeStruct((beams, widths.shape[0], count), jnp.float32),
        ],
        compiler_params=small,
        name="boxcar_peaks",
    )(widths, *arrived)
    return series, peaks.swapaxes(1, 2)


def solution(mesh):
    return jax.shard_map(
        lambda *arrays: tuple(local(*arrays)),
        mesh=mesh,
        in_specs=(
            P(None, "band", "trial"),
            P("band", None, None),
            P(),
            P("trial", None),
            P("trial", None),
            P(),
        ),
        out_specs=(P(None, ("trial", "band"), None), P(None, ("trial", "band"), None)),
        check_vma=False,
    )
```
